512 devices in a mesh: dp: 64 (over z, y), tensor: 8 (over x, core).
Axes of the slice: x: 4, y: 4, z: 16, core: 2. Of those that a mesh axis runs over, the one named last changes fastest.
Arguments:
- patches: bfloat16 [2048, 8, 3072], P('dp', None, 'tensor'), may hold values from -10 to 10
- counts: int32 [2048], P('dp'), may hold values from 1 to 8, as said below
- target: int32 [2048], P('dp'), may hold values from 0 to 63, as said below
- ln_gain: float32 [3072], replicated, may hold values from 0.25 to 1.75
- w_qkv: bfloat16 [3, 3072, 3072], P(None, 'dp', 'tensor'), may hold values from -1 to 1
- w_out: bfloat16 [3072, 3072], P('tensor', 'dp'), may hold values from -0.109375 to 0.109375
- cotangent: bfloat16 [2048, 8, 3072], P('dp', None, 'tensor'), may hold values from -6 to 6
Outputs:
- mixed: bfloat16 [2048, 8, 3072], P('dp', None, 'tensor')
- patch_grad: bfloat16 [2048, 8, 3072], P('dp', None, 'tensor')
The draws below stay inside these ranges and needn't reach their ends.
Inputs may be any that keep to these rules, and one draw needn't show every extreme that they name: `counts`: every draw has an image of 8 live patches and one of a single live patch. `target`: the 32 images of one source device go to 32 different devices, and every device receives exactly one image of each slot k.
All inputs are finite; a program needn't handle non-finite values.
Results may differ from the reference program's by a relative error of at most 0.014.
Values may be sent and summed in bfloat16 or wider, within the bound.
A program may use at most 64 MiB of HBM per device.

```python
import jax
import jax.numpy as jnp
from jax import lax

D = 3072
HEADS = 24
HD = 128
SLOT = 8
IMG_DEV = 32
IMAGES = 2048
N_DP = 64


def draw_patches(key, part):
    key = jax.random.fold_in(key, 31)
    values = jax.random.truncated_normal(jax.random.fold_in(key, 1), -6.0, 6.0, (IMAGES, SLOT, D), jnp.float32)
    return values.astype(jnp.bfloat16)


def draw_w_qkv(key, part):
    key = jax.random.fold_in(key, 37)
    values = jax.random.truncated_normal(jax.random.fold_in(key, 1), -6.0, 6.0, (3, D, HEADS * HD), jnp.float32)
    values = values * D ** (-0.5)
    return values.astype(jnp.bfloat16)


def draw_counts(key, part):
    key = jax.random.fold_in(key, 11)
    values = jax.random.randint(key, (IMAGES,), 1, SLOT + 1, dtype=jnp.int32)
    values = values.at[0].set(SLOT)
    return values.at[1].set(1)


def draw_target(key, part):
    key = jax.random.fold_in(key, 23)
    order = jax.random.permutation(jax.random.fold_in(key, 1), N_DP).astype(jnp.int32)
    offsets = jax.random.permutation(jax.random.fold_in(key, 2), N_DP).astype(jnp.int32)[:IMG_DEV]
    where_in = jnp.argsort(order, stable=True).astype(jnp.int32)
    source = jnp.arange(IMAGES, dtype=jnp.int32) // IMG_DEV
    slot_ids = jnp.arange(IMAGES, dtype=jnp.int32) % IMG_DEV
    return order[(where_in[source] + offsets[slot_ids]) % N_DP].astype(jnp.int32)


def shard_levels(stream_key, dims, cuts, low, high):
    gain, own = 1.0, jax.random.fold_in(stream_key, 6)
    for dim, shards_of in cuts:
        steps = jnp.exp(jax.random.uniform(jax.random.fold_in(own, dim), (shards_of,), jnp.float32, low / len(cuts), high / len(cuts)))
        gain = gain * jnp.repeat(steps, dims[dim] // shards_of).reshape([-1 if axis == dim else 1 for axis in range(len(dims))])
    return gain


def bell_draw(key, extent, width, most, cuts=(), kind=jnp.bfloat16):
    level = shard_levels(key, extent, cuts, -0.22, 0.18) if cuts else 1.0
    drawn = jax.random.normal(key, extent, jnp.float32) * width * level
    return jnp.minimum(jnp.maximum(drawn, -most), most).astype(kind)


def setup_inputs(seed: int = 0) -> dict:
    splits = jax.random.split(jax.random.key(seed), 8)
    return {
        "patches": draw_patches(jax.random.fold_in(splits[7], 71), 0),
        "counts": draw_counts(jax.random.fold_in(splits[7], 71), 0),
        "target": draw_target(jax.random.fold_in(splits[7], 71), 0),
        "ln_gain": jnp.clip(1.0 + 0.15 * jax.random.normal(splits[3], (D,), jnp.float32), 0.25, 1.75),
        "w_qkv": draw_w_qkv(jax.random.fold_in(splits[7], 71), 0),
        "w_out": bell_draw(splits[5], (HEADS * HD, D), (HEADS * HD) ** -0.5, 0.109375, ((0, 8), (1, 64))),
        "cotangent": bell_draw(splits[6], (IMAGES, SLOT, D), 1.0, 6.0, ((0, 64), (2, 8))),
    }


def normalize(rows):
    row_mean = lax.optimization_barrier(jnp.mean(rows, axis=-1, keepdims=True))
    centred = rows - row_mean
    inv_std = lax.rsqrt(lax.optimization_barrier(jnp.mean(centred * centred, axis=-1, keepdims=True)) + 1e-06)
    return (centred * inv_std, inv_std)

def reference(patches, counts, target, ln_gain, w_qkv, w_out, cotangent):
    slot_ids = jnp.arange(IMAGES, dtype=jnp.int32) % IMG_DEV
    dest_rows = (target * IMG_DEV + slot_ids).astype(jnp.int32)
    moved = jnp.zeros_like(patches).at[dest_rows].set(patches)
    moved_counts = jnp.zeros((IMAGES,), jnp.int32).at[dest_rows].set(counts)
    score_scale = HD ** (-0.5)

    def device_block(block):
        images, image_counts, grads_in = block
        total = IMG_DEV * SLOT
        rows_f = images.astype(jnp.float32).reshape(total, D)
        unit_rows, inv_std = normalize(rows_f)
        normed = (unit_rows * ln_gain).astype(jnp.bfloat16)
        shape4 = (IMG_DEV, SLOT, HEADS, HD)
        query = jnp.dot(normed, w_qkv[0], preferred_element_type=jnp.float32).astype(jnp.bfloat16).reshape(shape4)
        keys = jnp.dot(normed, w_qkv[1], preferred_element_type=jnp.float32).astype(jnp.bfloat16).reshape(shape4)
        values = jnp.dot(normed, w_qkv[2], preferred_element_type=jnp.float32).astype(jnp.bfloat16).reshape(shape4)
        q32, k32, v32 = (query.astype(jnp.float32), keys.astype(jnp.float32), values.astype(jnp.float32))
        positions = jnp.arange(SLOT, dtype=jnp.int32)
        key_ok = positions[None, :] < image_counts[:, None]
        row_ok = key_ok.reshape(total, 1)
        scores = jnp.einsum('ishd,ithd->ihst', q32, k32) * score_scale
        scores = jnp.where(key_ok[:, None, None, :], scores, -1e+30)
        top = lax.optimization_barrier(jnp.max(scores, axis=-1, keepdims=True))
        expo = jnp.exp(scores - top)
        probs = (expo / lax.optimization_barrier(jnp.sum(expo, axis=-1, keepdims=True))).astype(jnp.bfloat16)
        probs32 = probs.astype(jnp.float32)
        attn = jnp.einsum('ihst,ithd->ishd', probs32, v32).astype(jnp.bfloat16).reshape(total, HEADS * HD)
        branch = jnp.dot(attn, w_out, preferred_element_type=jnp.float32)
        mixed = jnp.where(row_ok, rows_f + branch, 0.0).astype(jnp.bfloat16)
        grad_rows = jnp.where(row_ok, grads_in.reshape(total, D), jnp.zeros((), jnp.bfloat16))
        attn_grad = jnp.dot(grad_rows, w_out.T, preferred_element_type=jnp.float32).astype(jnp.bfloat16)
        ag32 = attn_grad.reshape(shape4).astype(jnp.float32)
        dprobs = jnp.einsum('ishd,ithd->ihst', ag32, v32)
        value_grad = jnp.einsum('ihst,ishd->ithd', probs32, ag32).astype(jnp.bfloat16)
        inner = lax.optimization_barrier(jnp.sum(dprobs * probs32, axis=-1, keepdims=True))
        score_grad = (probs32 * (dprobs - inner) * score_scale).astype(jnp.bfloat16).astype(jnp.float32)
        query_grad = jnp.einsum('ihst,ithd->ishd', score_grad, k32).astype(jnp.bfloat16)
        key_grad = jnp.einsum('ihst,ishd->ithd', score_grad, q32).astype(jnp.bfloat16)
        flat = (total, HEADS * HD)
        normed_grad = jnp.dot(query_grad.reshape(flat), w_qkv[0].T, preferred_element_type=jnp.float32)
        normed_grad = normed_grad + jnp.dot(key_grad.reshape(flat), w_qkv[1].T, preferred_element_type=jnp.float32)
        normed_grad = normed_grad + jnp.dot(value_grad.reshape(flat), w_qkv[2].T, preferred_element_type=jnp.float32)
        scaled = normed_grad * ln_gain
        norm_back = inv_std * (scaled - lax.optimization_barrier(jnp.mean(scaled, axis=-1, keepdims=True)) - unit_rows * lax.optimization_barrier(jnp.mean(scaled * unit_rows, axis=-1, keepdims=True)))
        moved_grad = jnp.where(row_ok, grad_rows.astype(jnp.float32) + norm_back, 0.0).astype(jnp.bfloat16)
        return (mixed.reshape(IMG_DEV, SLOT, D), moved_grad.reshape(IMG_DEV, SLOT, D))
    blocks = (moved.reshape(N_DP, IMG_DEV, SLOT, D), moved_counts.reshape(N_DP, IMG_DEV), cotangent.reshape(N_DP, IMG_DEV, SLOT, D))
    mixed, moved_grad = lax.map(device_block, blocks)
    mixed = mixed.reshape(IMAGES, SLOT, D)
    patch_grad = moved_grad.reshape(IMAGES, SLOT, D)[dest_rows]
    return (mixed, patch_grad)
```

```python
import functools

import jax
import jax.numpy as jnp
from jax import lax
from jax.experimental import pallas as pl
from jax.experimental.pallas import tpu as pltpu
from jax.sharding import PartitionSpec as P

HD = 128
D = 3072
NZ, NY, NX = 16, 4, 4
ROWS = 256
W = 384
SHARD = 48
F32 = jnp.float32
BF16 = jnp.bfloat16
NT = (((1,), (1,)), ((), ()))
TN = (((0,), (0,)), ((), ()))
S_COT, S_XG, S_A1, S_M1, S_A2, S_M2 = 0, 7, 14, 29, 44, 47
S_AY, S_AZR, S_AZL = 50, 53, 61
S_BZR, S_BZL, S_BYR, S_BYL, S_BREL = 68, 76, 83, 99, 115
S_RS1, S_RS2, S_SC, S_R1, S_R2 = 131, 133, 139, 146, 149
N_SEM = 164


def dot(a, b, dims=(((1,), (0,)), ((), ()))):
    return lax.dot_general(a, b, dims, preferred_element_type=F32)


def block_kernel(
    meta_ref, x_ref, cot_ref, gain_ref, wqkv_ref, wout_ref, mixed_ref, pg_ref,
    wbuf, xg, cg, send, mid, mid2, recv, msend, mrecv, mall, pick, acc, uacc,
    part_o, part_n, sib_o, sib_n, q_o, q_n, rx_o, rx_n, scal, stats, ret1, got1, ret2, got2,
    ssem, rsem,
):
    dp = lax.axis_index("dp")
    tn = lax.axis_index("tensor")
    z, y = lax.div(dp, NY), lax.rem(dp, NY)
    x, c = lax.div(tn, 2), lax.rem(tn, 2)
    oc = 1 - c

    def at(dz=0, dy=0):
        return lax.rem(z + dz + NZ, NZ) * NY + lax.rem(y + dy + NY, NY)

    def tens(dx, core):
        return lax.rem(x + dx, NX) * 2 + core

    barrier = pltpu.get_barrier_semaphore()
    peers = [(at(k, 0), tn) for k in range(1, NZ)]
    peers += [(at(0, k), tn) for k in range(1, NY)]
    peers += [(dp, tens(k, c)) for k in range(1, NX)]
    peers += [(dp, tens(k, oc)) for k in range(NX)]
    for peer in peers:
        pl.semaphore_signal(barrier, inc=1, device_id=peer, device_id_type=pl.DeviceIdType.MESH)

    pending = []

    def copy(src, dst, sem, to):
        desc = pltpu.make_async_remote_copy(
            src_ref=src, dst_ref=dst, send_sem=ssem.at[sem], recv_sem=rsem.at[sem],
            device_id=to, device_id_type=pl.DeviceIdType.MESH,
        )
        desc.start()
        pending.append(desc)
        return desc

    wbuf[0:3, dp] = wqkv_ref[...]
    wbuf[3, dp] = wout_ref[...]
    cg[tn] = cot_ref[...]
    dest = meta_ref[0:1, :]
    slot = meta_ref[1:2, :]
    pack = (lax.broadcasted_iota(jnp.int32, (512, ROWS), 0) == dest).astype(BF16)
    sorted_rows = dot(pack, x_ref[...]).astype(BF16)
    send[...] = sorted_rows.reshape(NZ, 32, W)
    a_meta = jnp.where(
        lax.broadcasted_iota(jnp.int32, (NZ, ROWS), 0) == lax.shift_right_logical(dest, 5), slot + 1, 0
    ).astype(F32).astype(BF16)
    b_meta = (
        lax.broadcasted_iota(jnp.int32, (128, ROWS), 0) == lax.bitwise_and(dest, 31)
    ).astype(BF16)
    meta_rows = dot(a_meta, b_meta, NT)
    for k in range(NZ):
        msend[k] = meta_rows[k : k + 1, :]

    pl.semaphore_wait(barrier, len(peers))

    a_y = [copy(wbuf.at[3, dp], wbuf.at[3, dp], S_AY + k - 1, (at(0, k), tn)) for k in (1, 2, 3)]

    def b_zr(j):
        r = wbuf.at[pl.ds(0, 3), at(-j)]
        return copy(r, r, S_BZR + j, (at(1), tn))

    def b_zl(j):
        r = wbuf.at[pl.ds(0, 3), at(j)]
        return copy(r, r, S_BZL + j, (at(-1), tn))

    def b_y(d):
        r = wbuf.at[pl.ds(0, 3), at(d)]
        return copy(r, r, S_BYR + d, (at(0, 1), tn)), copy(r, r, S_BYL + d, (at(0, -1), tn))

    def b_relay(d, up):
        r = wbuf.at[pl.ds(0, 3), at(d, -1 if up else 1)]
        return copy(r, r, S_BREL + d, (at(0, 1 if up else -1), tn))

    def a_zr(j):
        r = wbuf.at[3, pl.ds(lax.rem(z - j + NZ, NZ) * NY, NY)]
        return copy(r, r, S_AZR + j, (at(1), tn))

    def a_zl(j):
        r = wbuf.at[3, pl.ds(lax.rem(z + j, NZ) * NY, NY)]
        return copy(r, r, S_AZL + j, (at(-1), tn))

    zr, zl, yy, rel, azr, azl = {}, {}, {}, {}, {}, {}
    zr[0], zl[0] = b_zr(0), b_zl(0)
    yy[0] = b_y(0)

    a1, m1 = [], []
    for k in range(1, NZ):
        p = lax.rem(z + k, NZ)
        m1.append(copy(msend.at[p], mrecv.at[z], S_M1 + k - 1, (at(k), tn)))
        a1.append(copy(send.at[p], mid.at[z], S_A1 + k - 1, (at(k), tn)))
    mid[z] = send[z]
    mrecv[z] = msend[z]

    def gather_start(buf, base):
        own = buf.at[tn]
        sib = copy(own, own, base, (dp, tens(0, oc)))
        return [sib] + [copy(own, own, base + k, (dp, tens(k, c))) for k in (1, 2, 3)]

    def gather_pass(buf, base, ds):
        out = []
        for k in (1, 2, 3):
            ds[k].wait_recv()
            r = buf.at[tens(NX - k, c)]
            out.append(copy(r, r, base + 3 + k, (dp, tens(0, oc))))
        return out

    cot_d = gather_start(cg, S_COT)
    a2, m2, xg_d, xg_f, cot_f = [], [], [], [], []

    def tiles_second():
        for d in a1 + m1:
            d.wait_recv()
        tiles = mid[...].astype(F32)
        for q in range(NY):
            mid2[q] = jnp.concatenate(
                [tiles[s, q * 8 : q * 8 + 8, :] for s in range(NZ)], axis=0
            ).astype(BF16)
        for k in (1, 2, 3):
            p = lax.rem(y + k, NY)
            m2.append(copy(mrecv, mall.at[y], S_M2 + k - 1, (at(0, k), tn)))
            a2.append(copy(mid2.at[p], recv.at[y], S_A2 + k - 1, (at(0, k), tn)))
        recv[y] = mid2[y]
        mall[y] = mrecv[...]

    def tiles_last():
        for d in a2 + m2:
            d.wait_recv()
        lane = lax.broadcasted_iota(jnp.int32, (128, 128), 1)
        sel = (
            lax.broadcasted_iota(jnp.int32, (128, 128), 0) == y * 8 + lax.bitwise_and(lane, 7)
        ).astype(BF16)
        mine = (
            lax.broadcasted_iota(jnp.int32, (NZ, 128), 0)
            == lax.shift_right_logical(lax.broadcasted_iota(jnp.int32, (NZ, 128), 1), 3)
        )
        parts = []
        for q in range(NY):
            rows = jnp.concatenate([mall[q, s] for s in range(NZ)], axis=0)
            t = dot(rows.astype(BF16), sel)
            parts.append(jnp.sum(jnp.where(mine, t, 0.0), axis=0, keepdims=True))
        where_to = jnp.concatenate(parts, axis=1).astype(jnp.int32) - 1
        picked = (lax.broadcasted_iota(jnp.int32, (ROWS, 512), 0) == where_to).astype(BF16)
        pick[...] = picked
        xg[tn] = dot(picked, recv[...].reshape(512, W)).astype(BF16)
        xg_d.extend(gather_start(xg, S_XG))

    for j in range(1, 9):
        zr[j - 1].wait_recv()
        if j < 8:
            zr[j] = b_zr(j)
        yy[NZ - j] = b_y(NZ - j)
        if j < 8:
            zl[j - 1].wait_recv()
            if j < 7:
                zl[j] = b_zl(j)
            yy[j] = b_y(j)
        if j == 1:
            for d in a_y:
                d.wait_recv()
            azr[0], azl[0] = a_zr(0), a_zl(0)
        else:
            azr[j - 2].wait_recv()
            azr[j - 1] = a_zr(j - 1)
            azl[j - 2].wait_recv()
            if j < 8:
                azl[j - 1] = a_zl(j - 1)
        if j == 1:
            yy[0][1].wait_recv()
            rel[0] = b_relay(0, False)
        else:
            d = NZ - (j - 1)
            yy[d][0].wait_recv()
            rel[d] = b_relay(d, True)
            d = j - 1
            yy[d][1].wait_recv()
            rel[d] = b_relay(d, False)
        if j == 3:
            cot_f = gather_pass(cg, S_COT, cot_d)
        if j == 4:
            tiles_second()
        if j == 5:
            tiles_last()
        if j == 7:
            xg_f = gather_pass(xg, S_XG, xg_d)
    yy[8][0].wait_recv()
    rel[8] = b_relay(8, True)

    xg_d[0].wait_recv()
    for d in xg_f:
        d.wait_recv()
    cot_d[0].wait_recv()
    for d in cot_f:
        d.wait_recv()
    total = jnp.zeros((ROWS, 1), F32)
    for t in range(8):
        total = total + jnp.sum(xg[t].astype(F32), axis=1, keepdims=True)
    mean = total * (1.0 / D)
    sq = jnp.zeros((ROWS, 1), F32)
    for t in range(8):
        cen = xg[t].astype(F32) - mean
        sq = sq + jnp.sum(cen * cen, axis=1, keepdims=True)
    inv_std = lax.rsqrt(sq * (1.0 / D) + 1e-06)
    live_col = jnp.sum(pick[...].astype(F32), axis=1, keepdims=True)
    eye = lax.broadcasted_iota(jnp.int32, (ROWS, ROWS), 0) == lax.broadcasted_iota(
        jnp.int32, (ROWS, ROWS), 1
    )
    live_row = jnp.sum(jnp.where(eye, live_col, 0.0), axis=0, keepdims=True)
    stats[0] = jnp.broadcast_to(mean, (ROWS, 128))
    stats[1] = jnp.broadcast_to(inv_std, (ROWS, 128))
    stats[2] = jnp.broadcast_to(live_col, (ROWS, 128))

    azr[7].wait_recv()
    for j in range(9):
        d = (NZ - j) % NZ
        if j > 0:
            yy[d][1].wait_recv()
            rel[d].wait_recv()
        if j < 8:
            yy[j][0].wait_recv()
            rel[j].wait_recv()

    acc[...] = jnp.zeros_like(acc)
    uacc[...] = jnp.zeros_like(uacc)

    def project(t, carry):
        m = stats[0][:, 0:1]
        inv = stats[1][:, 0:1]
        live = stats[2][:, 0:1]
        gain = gain_ref[t]
        normed = ((xg[t].astype(F32) - m) * inv * gain).astype(BF16)
        g0 = gain.astype(BF16)
        rest = gain - g0.astype(F32)
        g1 = rest.astype(BF16)
        g2 = (rest - g1.astype(F32)).astype(BF16)
        gains = jnp.concatenate(
            [g0.astype(F32), g1.astype(F32), g2.astype(F32), jnp.zeros((13, W), F32)], axis=0
        ).astype(BF16)
        for i in range(3):
            wt = wbuf[i, pl.ds(t * 8, 8)].reshape(W, W)
            acc[i] += dot(normed, wt)
            uacc[i] += dot(gains, wt)
        grad = jnp.where(live > 0.5, cg[t], jnp.zeros((), BF16))
        acc[3] += dot(grad, wbuf[3, pl.ds(t * 8, 8)].reshape(W, W))
        return carry

    lax.fori_loop(0, 8, project, 0)

    row_img = lax.shift_right_logical(lax.broadcasted_iota(jnp.int32, (ROWS, ROWS), 0), 3)
    col_img = lax.shift_right_logical(lax.broadcasted_iota(jnp.int32, (ROWS, ROWS), 1), 3)
    ok = (row_img == col_img) & (live_row > 0.5)
    scale = HD ** (-0.5)
    s1 = jnp.zeros((ROWS, 1), F32)
    s2 = jnp.zeros((ROWS, 1), F32)
    attn, grads = [], [[], [], []]
    for h in range(3):
        cols = slice(h * HD, (h + 1) * HD)
        qf, kf, vf = (acc[i][:, cols] for i in range(3))
        q, k, v = qf.astype(BF16), kf.astype(BF16), vf.astype(BF16)
        ag = acc[3][:, cols].astype(BF16)
        sc = jnp.where(ok, dot(q, k, NT) * scale, -1e30)
        ex = jnp.exp(sc - jnp.max(sc, axis=1, keepdims=True))
        probs = (ex / jnp.sum(ex, axis=1, keepdims=True)).astype(BF16)
        attn.append(dot(probs, v).astype(BF16))
        dprobs = dot(ag, v, NT)
        probs32 = probs.astype(F32)
        inner = jnp.sum(dprobs * probs32, axis=1, keepdims=True)
        sg = (probs32 * (dprobs - inner) * scale).astype(BF16)
        vg = dot(probs, ag, TN).astype(BF16)
        qg = dot(sg, k).astype(BF16)
        kg = dot(sg, q, TN).astype(BF16)
        for i, (g, f) in enumerate(((qg, qf), (kg, kf), (vg, vf))):
            grads[i].append(g)
            g32 = g.astype(F32)
            u = jnp.sum(uacc[i][:, cols], axis=0, keepdims=True)
            s1 = s1 + jnp.sum(g32 * u, axis=1, keepdims=True)
            s2 = s2 + jnp.sum(g32 * f, axis=1, keepdims=True)
    attn = jnp.concatenate(attn, axis=1)
    grads = [jnp.concatenate(g, axis=1) for g in grads]
    s1r = jnp.sum(jnp.where(eye, s1, 0.0), axis=0, keepdims=True)
    s2r = jnp.sum(jnp.where(eye, s2, 0.0), axis=0, keepdims=True)
    scal[tn] = jnp.concatenate([s1r, s2r, jnp.zeros((6, ROWS), F32)], axis=0)
    own_s = scal.at[tn]
    sc_d = [copy(own_s, own_s, S_SC + k - 1, (dp, tens(k, c))) for k in (1, 2, 3)]
    sc_d += [copy(own_s, own_s, S_SC + 3 + k, (dp, tens(k, oc))) for k in range(4)]

    for t in range(8):
        wts = [wbuf[i, t * 8 : t * 8 + 8].reshape(W, W) for i in range(3)]
        p = dot(grads[0], wts[0], NT) + dot(grads[1], wts[1], NT) + dot(grads[2], wts[2], NT)
        part_n[t % 2, t // 2] = p.astype(BF16)
    sib_nd = copy(part_n.at[oc], sib_n, S_RS1, (dp, tens(0, oc)))
    for t in range(8):
        part_o[t % 2, t // 2] = dot(
            attn, wbuf[3, t * 8 : t * 8 + 8].reshape(W, W), NT
        ).astype(BF16)
    sib_od = copy(part_o.at[oc], sib_o, S_RS1 + 1, (dp, tens(0, oc)))

    def fold(part, sib, q, rx, base):
        ds = []
        for k in (2, 1, 3):
            xx = lax.rem(x + k, NX)
            q[xx] = (part[c, xx].astype(F32) + sib[xx].astype(F32)).astype(BF16)
            ds.append(copy(q.at[xx], rx.at[k - 1], base + k - 1, (dp, tens(k, c))))
        return ds

    sib_nd.wait_recv()
    rs_n = fold(part_n, sib_n, q_n, rx_n, S_RS2)
    sib_od.wait_recv()
    rs_o = fold(part_o, sib_o, q_o, rx_o, S_RS2 + 3)

    def summed(part, sib, rx):
        s = part[c, x].astype(F32) + sib[x].astype(F32)
        return s + rx[0].astype(F32) + rx[1].astype(F32) + rx[2].astype(F32)

    for d in sc_d:
        d.wait_recv()
    sums = scal[0]
    for t in range(1, 8):
        sums = sums + scal[t]
    mean1 = jnp.sum(jnp.where(eye, sums[0:1, :], 0.0), axis=1, keepdims=True) * (1.0 / D)
    mean2 = jnp.sum(jnp.where(eye, sums[1:2, :], 0.0), axis=1, keepdims=True) * (1.0 / D)
    live = live_col > 0.5
    local = xg[tn].astype(F32)
    unit = (local - mean) * inv_std
    for d in rs_n:
        d.wait_recv()
    ng = summed(part_n, sib_n, rx_n)
    back = inv_std * (ng * gain_ref[tn] - mean1 - unit * mean2)
    moved = jnp.where(live, cot_ref[...].astype(F32) + back, 0.0).astype(BF16)

    ret1[...] = dot(pick[...], moved, TN).astype(BF16).reshape(NY, 128, W)
    r1 = []
    for k in (1, 2, 3):
        p = lax.rem(y + k, NY)
        r1.append(copy(ret1.at[p], got1.at[y], S_R1 + k - 1, (at(0, k), tn)))
    got1[y] = ret1[y]
    for d in r1:
        d.wait_recv()
    tiles = got1[...].astype(F32)
    for s in range(NZ):
        ret2[s] = jnp.concatenate(
            [tiles[q, s * 8 : s * 8 + 8, :] for q in range(NY)], axis=0
        ).astype(BF16)
    r2 = []
    for k in range(1, NZ):
        p = lax.rem(z + k, NZ)
        r2.append(copy(ret2.at[p], got2.at[z], S_R2 + k - 1, (at(k), tn)))
    got2[z] = ret2[z]

    for d in rs_o:
        d.wait_recv()
    branch = summed(part_o, sib_o, rx_o)
    mixed_ref[...] = jnp.where(live, local + branch, 0.0).astype(BF16)

    for d in r2:
        d.wait_recv()
    pack2 = (lax.broadcasted_iota(jnp.int32, (512, ROWS), 0) == meta_ref[0:1, :]).astype(BF16)
    pg_ref[...] = dot(pack2, got2[...].reshape(512, W), TN).astype(BF16)
    for d in pending:
        d.wait_send()


def per_device(patches, counts, target, ln_gain, w_qkv, w_out, cotangent):
    images, slot_len, width = patches.shape
    pos = jnp.arange(slot_len, dtype=jnp.int32)[None, :]
    dest = (target[:, None] * slot_len + pos).reshape(1, ROWS)
    ids = jnp.arange(images, dtype=jnp.int32)[:, None] * slot_len + pos
    slot = jnp.where(pos < counts[:, None], ids, -1).reshape(1, ROWS)
    meta = jnp.concatenate([dest, slot, jnp.zeros((6, ROWS), jnp.int32)], axis=0)
    vm = pl.BlockSpec(memory_space=pltpu.VMEM)
    b = lambda *s: pltpu.VMEM(s, BF16)
    f = lambda *s: pltpu.VMEM(s, F32)
    scratch = [
        b(4, 64, SHARD, W), b(8, ROWS, W), b(8, ROWS, W),
        b(NZ, 32, W), b(NZ, 32, W), b(NY, 128, W), b(NY, 128, W),
        f(NZ, 1, 128), f(NZ, 1, 128), f(NY, NZ, 1, 128),
        b(ROWS, 512), f(4, ROWS, W), f(3, 16, W),
        b(2, 4, ROWS, W), b(2, 4, ROWS, W), b(4, ROWS, W), b(4, ROWS, W),
        b(4, ROWS, W), b(4, ROWS, W), b(3, ROWS, W), b(3, ROWS, W),
        f(8, 8, ROWS), f(3, ROWS, 128),
        b(NY, 128, W), b(NY, 128, W), b(NZ, 32, W), b(NZ, 32, W),
        pltpu.SemaphoreType.DMA((N_SEM,)), pltpu.SemaphoreType.DMA((N_SEM,)),
    ]
    mixed, grad = pl.pallas_call(
        block_kernel,
        out_shape=[jax.ShapeDtypeStruct((ROWS, W), BF16)] * 2,
        in_specs=[vm] * 6,
        out_specs=[vm] * 2,
        scratch_shapes=scratch,
        compiler_params=pltpu.CompilerParams(
            collective_id=0, has_side_effects=True, vmem_limit_bytes=56 << 20
        ),
        name="attention_block",
    )(
        meta, patches.reshape(ROWS, width), cotangent.reshape(ROWS, width),
        ln_gain.reshape(8, 1, W), w_qkv, w_out.T,
    )
    return mixed.reshape(patches.shape), grad.reshape(patches.shape)


def solution(mesh):
    in_specs = (
        P("dp", None, "tensor"), P("dp"), P("dp"), P(), P(None, "dp", "tensor"),
        P("tensor", "dp"), P("dp", None, "tensor"),
    )
    out_specs = (P("dp", None, "tensor"), P("dp", None, "tensor"))
    return jax.shard_map(
        per_device, mesh=mesh, in_specs=in_specs, out_specs=out_specs, check_vma=False
    )
```

```python
import jax
import jax.numpy as jnp
from jax import lax
from jax.experimental import pallas as pl
from jax.experimental.pallas import tpu as pltpu
from jax.sharding import PartitionSpec as P

HD = 128
D = 3072
NZ, NY, NX = 16, 4, 4
ROWS = 256
W = 384
SHARD = 48
SLAB = 192
F32 = jnp.float32
BF16 = jnp.bfloat16
NT = (((1,), (1,)), ((), ()))
TN = (((0,), (0,)), ((), ()))
S_COT = 0
S_XG = 7
S_A1 = 14
S_M1 = 29
S_A2 = 44
S_M2 = 47
S_AY = 50
S_AZR = 53
S_AZL = 61
S_BZR = 68
S_BZL = 76
S_BYR = 83
S_BYL = 99
S_BREL = 115
S_NS = 131
S_NX = 135
S_OS = 144
S_OX = 145
S_SC = 148
S_R1 = 155
S_R2 = 164
N_SEM = 209


def dot(a, b, dims=(((1,), (0,)), ((), ()))):
    return lax.dot_general(a, b, dims, preferred_element_type=F32)


def block_kernel(
    meta_ref, x_ref, cot_ref, gain_ref, wqkv_ref, wout_ref, mixed_ref, pg_ref,
    wbuf, xg, cg, nb, gb, send, mid, mid2, recv, msend, mrecv, mall, pick, pick_t, pack_t,
    acc, part_n, part_o, sib_n, sib_o, q_n, q_o, rx_n, rx_o, scal,
    ret1, got1, ret2, got2,
    ssem, rsem,
):
    dp = lax.axis_index("dp")
    tn = lax.axis_index("tensor")
    z, y = lax.div(dp, NY), lax.rem(dp, NY)
    x, c = lax.div(tn, 2), lax.rem(tn, 2)
    oc = 1 - c

    def at(dz=0, dy=0):
        return lax.rem(z + dz + NZ, NZ) * NY + lax.rem(y + dy + NY, NY)

    def tens(dx, core):
        return lax.rem(x + dx, NX) * 2 + core

    barrier = pltpu.get_barrier_semaphore()
    peers = [(at(k, 0), tn) for k in range(1, NZ)]
    peers += [(at(0, k), tn) for k in range(1, NY)]
    peers += [(dp, tens(k, c)) for k in range(1, NX)]
    peers += [(dp, tens(k, oc)) for k in range(NX)]
    for peer in peers:
        pl.semaphore_signal(barrier, inc=1, device_id=peer, device_id_type=pl.DeviceIdType.MESH)

    pending = []

    def copy(src, dst, sem, to):
        desc = pltpu.make_async_remote_copy(
            src_ref=src, dst_ref=dst, send_sem=ssem.at[sem], recv_sem=rsem.at[sem],
            device_id=to, device_id_type=pl.DeviceIdType.MESH,
        )
        desc.start()
        pending.append(desc)
        return desc

    def rows_of(p):
        return pl.ds(pl.multiple_of(p * SHARD, SHARD), SHARD)

    def slab(zz):
        return pl.ds(pl.multiple_of(zz * SLAB, SLAB), SLAB)

    wbuf[0:3, rows_of(dp)] = wqkv_ref[...]
    wbuf[3, rows_of(dp)] = wout_ref[...]
    cg[tn] = cot_ref[...]
    eye = lax.broadcasted_iota(jnp.int32, (ROWS, ROWS), 0) == lax.broadcasted_iota(
        jnp.int32, (ROWS, ROWS), 1
    )
    pl.semaphore_wait(barrier, len(peers))

    def b_zr(j):
        r = wbuf.at[pl.ds(0, 3), rows_of(at(-j))]
        return copy(r, r, S_BZR + j, (at(1), tn))

    def b_zl(j):
        r = wbuf.at[pl.ds(0, 3), rows_of(at(j))]
        return copy(r, r, S_BZL + j, (at(-1), tn))

    def b_y(d):
        r = wbuf.at[pl.ds(0, 3), rows_of(at(d))]
        return copy(r, r, S_BYR + d, (at(0, 1), tn)), copy(r, r, S_BYL + d, (at(0, -1), tn))

    def b_relay(d, up):
        r = wbuf.at[pl.ds(0, 3), rows_of(at(d, -1 if up else 1))]
        return copy(r, r, S_BREL + d, (at(0, 1 if up else -1), tn))

    def a_zr(j):
        r = wbuf.at[3, slab(lax.rem(z - j + NZ, NZ))]
        return copy(r, r, S_AZR + j, (at(1), tn))

    def a_zl(j):
        r = wbuf.at[3, slab(lax.rem(z + j, NZ))]
        return copy(r, r, S_AZL + j, (at(-1), tn))

    zr, zl, yy, rel, azr, azl = {}, {}, {}, {}, {}, {}
    a_y, a1, m1, a2, m2, cot_d, cot_f, xg_d, xg_f = [], [], [], [], [], [], [], [], []

    def tiles_sort():
        dest = meta_ref[0:1, :]
        slot = meta_ref[1:2, :]
        pack = (lax.broadcasted_iota(jnp.int32, (512, ROWS), 0) == dest).astype(BF16)
        send[...] = dot(pack, x_ref[...]).astype(BF16).reshape(NZ, 32, W)
        pack_t[...] = dot(eye.astype(BF16), pack, NT).astype(BF16)
        a_meta = jnp.where(
            lax.broadcasted_iota(jnp.int32, (NZ, ROWS), 0) == lax.shift_right_logical(dest, 5),
            slot + 1, 0,
        ).astype(F32).astype(BF16)
        b_meta = (
            lax.broadcasted_iota(jnp.int32, (128, ROWS), 0) == lax.bitwise_and(dest, 31)
        ).astype(BF16)
        meta_rows = dot(a_meta, b_meta, NT)
        for k in range(NZ):
            msend[k] = meta_rows[k : k + 1, :]
        mid[z] = send[z]
        mrecv[z] = msend[z]

    def tiles_first(*ks):
        for k in ks:
            p = lax.rem(z + k, NZ)
            m1.append(copy(msend.at[p], mrecv.at[z], S_M1 + k - 1, (at(k), tn)))
            a1.append(copy(send.at[p], mid.at[z], S_A1 + k - 1, (at(k), tn)))

    def tiles_second():
        for d in a1 + m1:
            d.wait_recv()
        tiles = mid[...].astype(F32)
        for q in range(NY):
            mid2[q] = jnp.concatenate(
                [tiles[s, q * 8 : q * 8 + 8, :] for s in range(NZ)], axis=0
            ).astype(BF16)
        for k in (1, 2, 3):
            p = lax.rem(y + k, NY)
            m2.append(copy(mrecv, mall.at[y], S_M2 + k - 1, (at(0, k), tn)))
            a2.append(copy(mid2.at[p], recv.at[y], S_A2 + k - 1, (at(0, k), tn)))
        recv[y] = mid2[y]
        mall[y] = mrecv[...]

    def tiles_last():
        for d in a2 + m2:
            d.wait_recv()
        lane = lax.broadcasted_iota(jnp.int32, (128, 128), 1)
        sel = (
            lax.broadcasted_iota(jnp.int32, (128, 128), 0) == y * 8 + lax.bitwise_and(lane, 7)
        ).astype(BF16)
        mine = (
            lax.broadcasted_iota(jnp.int32, (NZ, 128), 0)
            == lax.shift_right_logical(lax.broadcasted_iota(jnp.int32, (NZ, 128), 1), 3)
        )
        parts = []
        for q in range(NY):
            rows = jnp.concatenate([mall[q, s] for s in range(NZ)], axis=0)
            t = dot(rows.astype(BF16), sel)
            parts.append(jnp.sum(jnp.where(mine, t, 0.0), axis=0, keepdims=True))
        where_to = jnp.concatenate(parts, axis=1).astype(jnp.int32) - 1
        picked = (lax.broadcasted_iota(jnp.int32, (ROWS, 512), 0) == where_to).astype(BF16)
        pick[...] = picked
        xg[tn] = dot(picked, recv[...].reshape(512, W)).astype(BF16)
        xg_d.extend(gather_start(xg, S_XG))
        eye512 = lax.broadcasted_iota(jnp.int32, (512, 512), 0) == lax.broadcasted_iota(
            jnp.int32, (512, 512), 1
        )
        pick_t[...] = dot(eye512.astype(BF16), picked, NT).astype(BF16)
        live_col = jnp.sum(picked.astype(F32), axis=1, keepdims=True)
        st["live_row"] = jnp.sum(jnp.where(eye, live_col, 0.0), axis=0, keepdims=True)
        st["live"] = live_col > 0.5

    def gather_start(buf, base):
        own = buf.at[tn]
        sib = copy(own, own, base, (dp, tens(0, oc)))
        return [sib] + [copy(own, own, base + k, (dp, tens(k, c))) for k in (1, 2, 3)]

    def gather_pass(buf, base, ds):
        out = []
        for k in (1, 2, 3):
            ds[k].wait_recv()
            r = buf.at[tens(NX - k, c)]
            out.append(copy(r, r, base + 3 + k, (dp, tens(0, oc))))
        return out

    def a_first():
        for k in (1, 2, 3):
            r = wbuf.at[3, rows_of(dp)]
            a_y.append(copy(r, r, S_AY + k - 1, (at(0, k), tn)))

    def b_step(j):
        if j == 0:
            zr[0], zl[0] = b_zr(0), b_zl(0)
            yy[0] = b_y(0)
            return
        zr[j - 1].wait_recv()
        if j < 8:
            zr[j] = b_zr(j)
        yy[NZ - j] = b_y(NZ - j)
        if j < 8:
            zl[j - 1].wait_recv()
            if j < 7:
                zl[j] = b_zl(j)
            yy[j] = b_y(j)

    def relay_step(j):
        if j > 0:
            d = NZ - j
            yy[d][0].wait_recv()
            rel[d] = b_relay(d, True)
        if j < 8:
            yy[j][1].wait_recv()
            rel[j] = b_relay(j, False)

    def a_step(j):
        if j == 0:
            for d in a_y:
                d.wait_recv()
        else:
            azr[j - 1].wait_recv()
            if j < 8:
                azl[j - 1].wait_recv()
        if j < 8:
            azr[j] = a_zr(j)
        if j < 7:
            azl[j] = a_zl(j)

    def b_done(j):
        d = (NZ - j) % NZ
        if j > 0:
            yy[d][1].wait_recv()
            rel[d].wait_recv()
        if j < 8:
            yy[j][0].wait_recv()
            rel[j].wait_recv()

    def project_qkv(j):
        b_done(j)
        for zz in {0: (z,), 8: (lax.rem(z + 8, NZ),)}.get(
            j, (lax.rem(z + j, NZ), lax.rem(z - j + NZ, NZ))
        ):
            rows = nb[zz]
            for i in range(3):
                p = dot(rows, wbuf[i, slab(zz)])
                acc[i] = p if j == 0 else acc[i] + p

    def project_grad(j):
        for zz in {0: (z,), 8: (lax.rem(z + 8, NZ),)}.get(
            j, (lax.rem(z + j, NZ), lax.rem(z - j + NZ, NZ))
        ):
            p = dot(gb[zz], wbuf[3, slab(zz)])
            acc[3, 0:ROWS] = p if j == 0 else acc[3, 0:ROWS] + p

    def grads_ready():
        cot_d[0].wait_recv()
        for d in cot_f:
            d.wait_recv()
        for t in range(8):
            g = jnp.where(st["live"], cg[t], jnp.zeros((), BF16))
            gb[2 * t] = g[:, :SLAB]
            gb[2 * t + 1] = g[:, SLAB:]

    def norm():
        xg_d[0].wait_recv()
        for d in xg_f:
            d.wait_recv()
        total = jnp.zeros((ROWS, 1), F32)
        for t in range(8):
            total = total + jnp.sum(xg[t].astype(F32), axis=1, keepdims=True)
        mean = total * (1.0 / D)
        sq = jnp.zeros((ROWS, 1), F32)
        for t in range(8):
            cen = xg[t].astype(F32) - mean
            sq = sq + jnp.sum(cen * cen, axis=1, keepdims=True)
        inv_std = lax.rsqrt(sq * (1.0 / D) + 1e-06)
        for t in range(8):
            gain = gain_ref[t]
            normed = ((xg[t].astype(F32) - mean) * inv_std * gain).astype(BF16)
            g0 = gain.astype(BF16).astype(F32)
            g1 = (gain - g0).astype(BF16).astype(F32)
            g2 = (gain - g0 - g1).astype(BF16).astype(F32)
            gains = jnp.concatenate([g0, g1, g2, jnp.zeros((13, W), F32)], axis=0).astype(BF16)
            for half in range(2):
                lanes = slice(half * SLAB, (half + 1) * SLAB)
                nb[2 * t + half, 0:ROWS] = normed[:, lanes]
                nb[2 * t + half, ROWS:] = gains[:, lanes]
        st["mean"], st["inv_std"] = mean, inv_std

    st = {}

    def cot_start():
        cot_d.extend(gather_start(cg, S_COT))

    def cot_pass():
        cot_f.extend(gather_pass(cg, S_COT, cot_d))

    def x_pass():
        xg_f.extend(gather_pass(xg, S_XG, xg_d))

    b_step(0)
    a_first()
    cot_start()
    tiles_sort()
    tiles_first(8,7,9,6,10)
    b_step(1)
    tiles_first(5,11,4,12,3)
    relay_step(0)
    b_step(2)
    tiles_first(13,2,14,1,15)
    relay_step(1)
    a_step(0)
    b_step(3)
    relay_step(2)
    a_step(1)
    b_step(4)
    cot_pass()
    tiles_second()
    relay_step(3)
    a_step(2)
    b_step(5)
    relay_step(4)
    a_step(3)
    b_step(6)
    tiles_last()
    relay_step(5)
    a_step(4)
    b_step(7)
    grads_ready()
    relay_step(6)
    a_step(5)
    x_pass()
    b_step(8)
    norm()
    relay_step(7)
    a_step(6)
    project_qkv(0)
    project_qkv(1)
    relay_step(8)
    project_qkv(2)
    a_step(7)
    project_qkv(3)
    project_qkv(4)
    a_step(8)
    project_qkv(5)
    project_qkv(6)
    for j in range(9):
        project_grad(j)
    project_qkv(7)
    project_qkv(8)
    live, live_row, mean, inv_std = st["live"], st["live_row"], st["mean"], st["inv_std"]

    half_rows = ROWS // 2
    row_img = lax.shift_right_logical(
        lax.broadcasted_iota(jnp.int32, (half_rows, half_rows), 0), 3
    )
    col_img = lax.shift_right_logical(
        lax.broadcasted_iota(jnp.int32, (half_rows, half_rows), 1), 3
    )
    same = row_img == col_img
    scale = HD ** (-0.5)
    attn_rows, grad_rows, s1_rows, s2_rows = [], [], [], []
    for r in range(2):
        rs = slice(r * half_rows, (r + 1) * half_rows)
        ok = same & (live_row[:, rs] > 0.5)
        s1 = jnp.zeros((half_rows, 1), F32)
        s2 = jnp.zeros((half_rows, 1), F32)
        attn, grads = [], [[], [], []]
        for h in range(3):
            cols = slice(h * HD, (h + 1) * HD)
            qf, kf, vf = (acc[i, rs, cols] for i in range(3))
            q, k, v = qf.astype(BF16), kf.astype(BF16), vf.astype(BF16)
            ag = acc[3, rs, cols].astype(BF16)
            sc = jnp.where(ok, dot(q, k, NT) * scale, -1e30)
            ex = jnp.exp(sc - jnp.max(sc, axis=1, keepdims=True))
            probs = (ex / jnp.sum(ex, axis=1, keepdims=True)).astype(BF16)
            attn.append(dot(probs, v).astype(BF16))
            dprobs = dot(ag, v, NT)
            probs32 = probs.astype(F32)
            inner = jnp.sum(dprobs * probs32, axis=1, keepdims=True)
            sg = (probs32 * (dprobs - inner) * scale).astype(BF16)
            vg = dot(probs, ag, TN).astype(BF16)
            qg = dot(sg, k).astype(BF16)
            kg = dot(sg, q, TN).astype(BF16)
            for i, (g, f) in enumerate(((qg, qf), (kg, kf), (vg, vf))):
                grads[i].append(g)
                g32 = g.astype(F32)
                u = jnp.sum(acc[i, ROWS:, cols], axis=0, keepdims=True)
                s1 = s1 + jnp.sum(g32 * u, axis=1, keepdims=True)
                s2 = s2 + jnp.sum(g32 * f, axis=1, keepdims=True)
        attn_rows.append(jnp.concatenate(attn, axis=1))
        grad_rows.append([jnp.concatenate(g, axis=1) for g in grads])
        s1_rows.append(s1)
        s2_rows.append(s2)
    attn = jnp.concatenate(attn_rows, axis=0)
    grads = [jnp.concatenate([g[i] for g in grad_rows], axis=0) for i in range(3)]

    sib_nd = {}
    for xx in range(NX):
        for cc in range(2):
            t = xx * 2 + cc
            wts = [wbuf[i, t * W : t * W + W] for i in range(3)]
            p = dot(grads[0], wts[0], NT) + dot(grads[1], wts[1], NT) + dot(grads[2], wts[2], NT)
            for n in range(3):
                part_n[cc, xx, n] = p[:, n * 128 : n * 128 + 128].astype(BF16)
        sib_nd[xx] = copy(part_n.at[oc, xx], sib_n.at[xx], S_NS + xx, (dp, tens(0, oc)))
    s1r = jnp.sum(jnp.where(eye, jnp.concatenate(s1_rows, axis=0), 0.0), axis=0, keepdims=True)
    s2r = jnp.sum(jnp.where(eye, jnp.concatenate(s2_rows, axis=0), 0.0), axis=0, keepdims=True)
    scal[tn] = jnp.concatenate([s1r, s2r, jnp.zeros((6, ROWS), F32)], axis=0)
    own_s = scal.at[tn]
    sc_d = [copy(own_s, own_s, S_SC + k - 1, (dp, tens(k, c))) for k in (1, 2, 3)]
    sc_d += [copy(own_s, own_s, S_SC + 3 + k, (dp, tens(k, oc))) for k in range(4)]
    for t in range(8):
        part_o[t % 2, t // 2] = dot(attn, wbuf[3, t * W : t * W + W], NT).astype(BF16)
    sib_od = copy(part_o.at[oc], sib_o, S_OS, (dp, tens(0, oc)))

    for xx in range(NX):
        sib_nd[xx].wait_recv()
    rs_n = {}
    for n in range(3):
        for k in (2, 1, 3):
            xx = lax.rem(x + k, NX)
            q_n[xx, n] = (part_n[c, xx, n].astype(F32) + sib_n[xx, n].astype(F32)).astype(BF16)
            rs_n[n, k] = copy(
                q_n.at[xx, n], rx_n.at[k - 1, n], S_NX + n * 3 + k - 1, (dp, tens(k, c))
            )

    local = xg[tn].astype(F32)
    unit = (local - mean) * inv_std
    for d in sc_d:
        d.wait_recv()
    sums = scal[0]
    for t in range(1, 8):
        sums = sums + scal[t]
    mean1 = jnp.sum(jnp.where(eye, sums[0:1, :], 0.0), axis=1, keepdims=True) * (1.0 / D)
    mean2 = jnp.sum(jnp.where(eye, sums[1:2, :], 0.0), axis=1, keepdims=True) * (1.0 / D)

    r1, r2, rs_o = {}, {}, {}

    def return_y(n):
        lanes = slice(n * 128, n * 128 + 128)
        ng = part_n[c, x, n].astype(F32) + sib_n[x, n].astype(F32)
        for k in (1, 2, 3):
            rs_n[n, k].wait_recv()
            ng = ng + rx_n[k - 1, n].astype(F32)
        back = inv_std * (ng * gain_ref[tn][:, lanes] - mean1 - unit[:, lanes] * mean2)
        moved = jnp.where(live, cot_ref[:, lanes].astype(F32) + back, 0.0).astype(BF16)
        ret1[n] = dot(pick_t[...], moved).astype(BF16).reshape(NY, 128, 128)
        for k in (1, 2, 3):
            p = lax.rem(y + k, NY)
            r1[n, k] = copy(ret1.at[n, p], got1.at[n, y], S_R1 + n * 3 + k - 1, (at(0, k), tn))
        got1[n, y] = ret1[n, y]

    def return_z(n):
        for k in (1, 2, 3):
            r1[n, k].wait_recv()
        tiles = got1[n].astype(F32)
        for s in range(NZ):
            ret2[n, s] = jnp.concatenate(
                [tiles[q, s * 8 : s * 8 + 8, :] for q in range(NY)], axis=0
            ).astype(BF16)
        for k in (8, 7, 9, 6, 10, 5, 11, 4, 12, 3, 13, 2, 14, 1, 15):
            p = lax.rem(z + k, NZ)
            r2[n, k] = copy(ret2.at[n, p], got2.at[n, z], S_R2 + n * 15 + k - 1, (at(k), tn))
        got2[n, z] = ret2[n, z]

    def return_last(n):
        for k in range(1, NZ):
            r2[n, k].wait_recv()
        pg_ref[:, n * 128 : n * 128 + 128] = dot(
            pack_t[...], got2[n].reshape(512, 128)
        ).astype(BF16)

    return_y(0)
    return_y(1)
    return_z(0)
    return_y(2)
    return_z(1)
    sib_od.wait_recv()
    for k in (2, 1, 3):
        xx = lax.rem(x + k, NX)
        q_o[xx] = (part_o[c, xx].astype(F32) + sib_o[xx].astype(F32)).astype(BF16)
        rs_o[k] = copy(q_o.at[xx], rx_o.at[k - 1], S_OX + k - 1, (dp, tens(k, c)))
    return_z(2)
    branch = part_o[c, x].astype(F32) + sib_o[x].astype(F32)
    for k in (1, 2, 3):
        rs_o[k].wait_recv()
        branch = branch + rx_o[k - 1].astype(F32)
    mixed_ref[...] = jnp.where(live, local + branch, 0.0).astype(BF16)
    for n in range(3):
        return_last(n)
    for d in pending:
        d.wait_send()


def per_device(patches, counts, target, ln_gain, w_qkv, w_out, cotangent):
    images, slot_len, width = patches.shape
    pos = jnp.arange(slot_len, dtype=jnp.int32)[None, :]
    dest = (target[:, None] * slot_len + pos).reshape(1, ROWS)
    ids = jnp.arange(images, dtype=jnp.int32)[:, None] * slot_len + pos
    slot = jnp.where(pos < counts[:, None], ids, -1).reshape(1, ROWS)
    meta = jnp.concatenate([dest, slot, jnp.zeros((6, ROWS), jnp.int32)], axis=0)
    vm = pl.BlockSpec(memory_space=pltpu.VMEM)
    b = lambda *s: pltpu.VMEM(s, BF16)
    f = lambda *s: pltpu.VMEM(s, F32)
    scratch = [
        b(4, D, W), b(8, ROWS, W), b(8, ROWS, W), b(NZ, ROWS + 16, SLAB), b(NZ, ROWS, SLAB),
        b(NZ, 32, W), b(NZ, 32, W), b(NY, 128, W), b(NY, 128, W),
        f(NZ, 1, 128), f(NZ, 1, 128), f(NY, NZ, 1, 128),
        b(ROWS, 512), b(512, ROWS), b(ROWS, 512), f(4, ROWS + 16, W),
        b(2, 4, 3, ROWS, 128), b(2, 4, ROWS, W), b(4, 3, ROWS, 128), b(4, ROWS, W),
        b(4, 3, ROWS, 128), b(4, ROWS, W), b(3, 3, ROWS, 128), b(3, ROWS, W), f(8, 8, ROWS),
        b(3, NY, 128, 128), b(3, NY, 128, 128), b(3, NZ, 32, 128), b(3, NZ, 32, 128),
        pltpu.SemaphoreType.DMA((N_SEM,)), pltpu.SemaphoreType.DMA((N_SEM,)),
    ]
    mixed, grad = pl.pallas_call(
        block_kernel,
        out_shape=[jax.ShapeDtypeStruct((ROWS, W), BF16)] * 2,
        in_specs=[vm] * 6,
        out_specs=[vm] * 2,
        scratch_shapes=scratch,
        compiler_params=pltpu.CompilerParams(
            collective_id=0, has_side_effects=True, vmem_limit_bytes=56 << 20
        ),
        name="attention_block",
    )(
        meta, patches.reshape(ROWS, width), cotangent.reshape(ROWS, width),
        ln_gain.reshape(8, 1, W), w_qkv, w_out.T,
    )
    return mixed.reshape(patches.shape), grad.reshape(patches.shape)


def solution(mesh):
    in_specs = (
        P("dp", None, "tensor"), P("dp"), P("dp"), P(), P(None, "dp", "tensor"),
        P("tensor", "dp"), P("dp", None, "tensor"),
    )
    out_specs = (P("dp", None, "tensor"), P("dp", None, "tensor"))
    return jax.shard_map(
        per_device, mesh=mesh, in_specs=in_specs, out_specs=out_specs, check_vma=False
    )
```

```python
import jax
import jax.numpy as jnp
from jax import lax
from jax.experimental import pallas as pl
from jax.experimental.pallas import tpu as pltpu
from jax.sharding import PartitionSpec as P

HD = 128
D = 3072
NZ, NY, NX = 16, 4, 4
ROWS = 256
W = 384
SHARD = 48
SLAB = 192
F32 = jnp.float32
BF16 = jnp.bfloat16
NT = (((1,), (1,)), ((), ()))
TN = (((0,), (0,)), ((), ()))
S_COT = 0
S_XG = 7
S_A1 = 14
S_M1 = 17
S_A2 = 20
S_M2 = 35
S_AY = 50
S_AZR = 53
S_AZL = 61
S_BZR = 68
S_BZL = 76
S_BYR = 83
S_BYL = 99
S_BREL = 115
S_NS = 131
S_NX = 134
S_OS = 143
S_OX = 144
S_SC = 147
S_R1 = 154
S_R2 = 199
N_SEM = 208


def dot(a, b, dims=(((1,), (0,)), ((), ()))):
    return lax.dot_general(a, b, dims, preferred_element_type=F32)


def block_kernel(
    target_ref, counts_ref, x_hbm, cot_hbm, gain_hbm, wqkv_hbm, wout_hbm, mixed_ref, pg_ref,
    x_ref, cot_ref, gain_ref, wbuf, xg, cg, nb, gb, send, mid, mid2, recv, msend, mrecv, mall,
    pick, pick_t, pack_t, acc, part_n, part_o, sib_n, sib_o, q_n, q_o, rx_n, rx_o, scal,
    ret1, got1, ret2, got2, ssem, rsem, lsem,
):
    dp = lax.axis_index("dp")
    tn = lax.axis_index("tensor")
    z, y = lax.div(dp, NY), lax.rem(dp, NY)
    x, c = lax.div(tn, 2), lax.rem(tn, 2)
    oc = 1 - c

    def at(dz=0, dy=0):
        return lax.rem(z + dz + NZ, NZ) * NY + lax.rem(y + dy + NY, NY)

    def tens(dx, core):
        return lax.rem(x + dx, NX) * 2 + core

    def rows_of(p):
        return pl.ds(pl.multiple_of(p * SHARD, SHARD), SHARD)

    def slab(zz):
        return pl.ds(pl.multiple_of(zz * SLAB, SLAB), SLAB)

    barrier = pltpu.get_barrier_semaphore()
    peers = [(at(k, 0), tn) for k in range(1, NZ)]
    peers += [(at(0, k), tn) for k in range(1, NY)]
    peers += [(dp, tens(k, c)) for k in range(1, NX)]
    peers += [(dp, tens(k, oc)) for k in range(NX)]
    for peer in peers:
        pl.semaphore_signal(barrier, inc=1, device_id=peer, device_id_type=pl.DeviceIdType.MESH)
    loads = []
    for i, (a, b) in enumerate((
        (wqkv_hbm, wbuf.at[pl.ds(0, 3), rows_of(dp)]), (wout_hbm, wbuf.at[3, rows_of(dp)]),
        (cot_hbm, cg.at[tn]), (x_hbm, x_ref), (cot_hbm, cot_ref), (gain_hbm, gain_ref),
    )):
        loads.append(pltpu.make_async_copy(a, b, lsem.at[i]))
        loads[-1].start()

    pending = []

    def copy(src, dst, sem, to):
        desc = pltpu.make_async_remote_copy(
            src_ref=src, dst_ref=dst, send_sem=ssem.at[sem], recv_sem=rsem.at[sem],
            device_id=to, device_id_type=pl.DeviceIdType.MESH,
        )
        desc.start()
        pending.append(desc)
        return desc

    eye = lax.broadcasted_iota(jnp.int32, (ROWS, ROWS), 0) == lax.broadcasted_iota(
        jnp.int32, (ROWS, ROWS), 1
    )
    for d in loads:
        d.wait()
    pl.semaphore_wait(barrier, len(peers))

    def b_zr(j):
        r = wbuf.at[pl.ds(0, 3), rows_of(at(-j))]
        return copy(r, r, S_BZR + j, (at(1), tn))

    def b_zl(j):
        r = wbuf.at[pl.ds(0, 3), rows_of(at(j))]
        return copy(r, r, S_BZL + j, (at(-1), tn))

    def b_y(d):
        r = wbuf.at[pl.ds(0, 3), rows_of(at(d))]
        return copy(r, r, S_BYR + d, (at(0, 1), tn)), copy(r, r, S_BYL + d, (at(0, -1), tn))

    def b_relay(d, up):
        r = wbuf.at[pl.ds(0, 3), rows_of(at(d, -1 if up else 1))]
        return copy(r, r, S_BREL + d, (at(0, 1 if up else -1), tn))

    def a_zr(j):
        r = wbuf.at[3, slab(lax.rem(z - j + NZ, NZ))]
        return copy(r, r, S_AZR + j, (at(1), tn))

    def a_zl(j):
        r = wbuf.at[3, slab(lax.rem(z + j, NZ))]
        return copy(r, r, S_AZL + j, (at(-1), tn))

    zr, zl, yy, rel, azr, azl = {}, {}, {}, {}, {}, {}
    a_y, a1, m1, a2, m2, cot_d, cot_f, xg_d, xg_f = [], [], [], [], [], [], [], [], []

    def tiles_sort():
        spread = (
            lax.shift_right_logical(lax.broadcasted_iota(jnp.int32, (32, ROWS), 1), 3)
            == lax.broadcasted_iota(jnp.int32, (32, ROWS), 0)
        ).astype(BF16)
        pair = jnp.concatenate(
            [target_ref[...].astype(F32), counts_ref[...].astype(F32), jnp.zeros((14, 32), F32)],
            axis=0,
        ).astype(BF16)
        pair = dot(pair, spread).astype(jnp.int32)
        lane = lax.broadcasted_iota(jnp.int32, (1, ROWS), 1)
        row = lax.bitwise_and(lane, 7)
        to = pair[0:1, :]
        dest = lax.bitwise_and(to, 3) * 128 + lax.shift_right_logical(to, 2) * 8 + row
        slot = jnp.where(row < pair[1:2, :], lane, -1)
        pack = (lax.broadcasted_iota(jnp.int32, (512, ROWS), 0) == dest).astype(BF16)
        send[...] = dot(pack, x_ref[...]).astype(BF16).reshape(NY, 128, W)
        a_meta = jnp.where(
            lax.broadcasted_iota(jnp.int32, (16, ROWS), 0) == lax.shift_right_logical(dest, 7),
            slot + 1, 0,
        ).astype(F32).astype(BF16)
        b_meta = (
            lax.broadcasted_iota(jnp.int32, (128, ROWS), 0) == lax.bitwise_and(dest, 127)
        ).astype(BF16)
        meta_rows = dot(a_meta, b_meta, NT)
        for k in range(NY):
            msend[k] = meta_rows[k : k + 1, :]
        for k in (1, 2, 3):
            p = lax.rem(y + k, NY)
            m1.append(copy(msend.at[p], mrecv.at[y], S_M1 + k - 1, (at(0, k), tn)))
            a1.append(copy(send.at[p], mid.at[y], S_A1 + k - 1, (at(0, k), tn)))
        mid[y] = send[y]
        mrecv[y] = msend[y]
        pack_t[...] = dot(eye.astype(BF16), pack, NT).astype(BF16)

    def tiles_second():
        for d in a1 + m1:
            d.wait_recv()
        tiles = mid[...].astype(F32)
        for q in range(NZ):
            mid2[q] = jnp.concatenate(
                [tiles[s, q * 8 : q * 8 + 8, :] for s in range(NY)], axis=0
            ).astype(BF16)
        recv[z] = mid2[z]
        mall[z] = mrecv[...]

    def tiles_z(*ks):
        for k in ks:
            p = lax.rem(z + k, NZ)
            m2.append(copy(mrecv, mall.at[z], S_M2 + k - 1, (at(k), tn)))
            a2.append(copy(mid2.at[p], recv.at[z], S_A2 + k - 1, (at(k), tn)))

    def tiles_last():
        for d in a2 + m2:
            d.wait_recv()
        lane = lax.broadcasted_iota(jnp.int32, (128, 512), 1)
        sel = (
            lax.broadcasted_iota(jnp.int32, (128, 512), 0) == z * 8 + lax.bitwise_and(lane, 7)
        ).astype(BF16)
        mine = (
            lax.broadcasted_iota(jnp.int32, (64, 512), 0)
            == lax.shift_right_logical(lax.broadcasted_iota(jnp.int32, (64, 512), 1), 3)
        )
        rows = jnp.concatenate([mall[q, s] for q in range(NZ) for s in range(NY)], axis=0)
        where_to = jnp.sum(
            jnp.where(mine, dot(rows.astype(BF16), sel), 0.0), axis=0, keepdims=True
        ).astype(jnp.int32) - 1
        picked = (lax.broadcasted_iota(jnp.int32, (ROWS, 512), 0) == where_to).astype(BF16)
        pick[...] = picked
        xg[tn] = dot(picked, recv[...].reshape(512, W)).astype(BF16)
        xg_d.extend(gather_start(xg, S_XG))

    def tiles_after():
        eye512 = lax.broadcasted_iota(jnp.int32, (512, 512), 0) == lax.broadcasted_iota(
            jnp.int32, (512, 512), 1
        )
        pick_t[...] = dot(eye512.astype(BF16), pick[...], NT).astype(BF16)
        live_col = jnp.sum(pick[...].astype(F32), axis=1, keepdims=True)
        st["live_row"] = jnp.sum(jnp.where(eye, live_col, 0.0), axis=0, keepdims=True)
        st["live"] = live_col > 0.5

    def gather_start(buf, base):
        own = buf.at[tn]
        sib = copy(own, own, base, (dp, tens(0, oc)))
        return [sib] + [copy(own, own, base + k, (dp, tens(k, c))) for k in (1, 2, 3)]

    def gather_pass(buf, base, ds):
        out = []
        for k in (1, 2, 3):
            ds[k].wait_recv()
            r = buf.at[tens(NX - k, c)]
            out.append(copy(r, r, base + 3 + k, (dp, tens(0, oc))))
        return out

    def a_first():
        for k in (1, 2, 3):
            r = wbuf.at[3, rows_of(dp)]
            a_y.append(copy(r, r, S_AY + k - 1, (at(0, k), tn)))

    def b_step(j):
        if j == 0:
            zr[0], zl[0] = b_zr(0), b_zl(0)
            yy[0] = b_y(0)
            return
        zr[j - 1].wait_recv()
        if j < 8:
            zr[j] = b_zr(j)
        yy[NZ - j] = b_y(NZ - j)
        if j < 8:
            zl[j - 1].wait_recv()
            if j < 7:
                zl[j] = b_zl(j)
            yy[j] = b_y(j)

    def relay_step(j):
        if j > 0:
            d = NZ - j
            yy[d][0].wait_recv()
            rel[d] = b_relay(d, True)
        if j < 8:
            yy[j][1].wait_recv()
            rel[j] = b_relay(j, False)

    def a_step(j):
        if j == 0:
            for d in a_y:
                d.wait_recv()
        else:
            azr[j - 1].wait_recv()
            if j < 8:
                azl[j - 1].wait_recv()
        if j < 8:
            azr[j] = a_zr(j)
        if j < 7:
            azl[j] = a_zl(j)

    def b_done(j):
        d = (NZ - j) % NZ
        if j > 0:
            yy[d][1].wait_recv()
            rel[d].wait_recv()
        if j < 8:
            yy[j][0].wait_recv()
            rel[j].wait_recv()

    def project_qkv(j):
        b_done(j)
        for zz in {0: (z,), 8: (lax.rem(z + 8, NZ),)}.get(
            j, (lax.rem(z + j, NZ), lax.rem(z - j + NZ, NZ))
        ):
            rows = nb[zz]
            for i in range(3):
                p = dot(rows, wbuf[i, slab(zz)])
                acc[i] = p if j == 0 else acc[i] + p

    def project_grad(j):
        for zz in {0: (z,), 8: (lax.rem(z + 8, NZ),)}.get(
            j, (lax.rem(z + j, NZ), lax.rem(z - j + NZ, NZ))
        ):
            p = dot(gb[zz], wbuf[3, slab(zz)])
            acc[3, 0:ROWS] = p if j == 0 else acc[3, 0:ROWS] + p

    def grads_ready():
        cot_d[0].wait_recv()
        for d in cot_f:
            d.wait_recv()
        for t in range(8):
            g = jnp.where(st["live"], cg[t], jnp.zeros((), BF16))
            gb[2 * t] = g[:, :SLAB]
            gb[2 * t + 1] = g[:, SLAB:]

    def norm():
        xg_d[0].wait_recv()
        for d in xg_f:
            d.wait_recv()
        total = jnp.zeros((ROWS, 1), F32)
        for t in range(8):
            total = total + jnp.sum(xg[t].astype(F32), axis=1, keepdims=True)
        mean = total * (1.0 / D)
        sq = jnp.zeros((ROWS, 1), F32)
        for t in range(8):
            cen = xg[t].astype(F32) - mean
            sq = sq + jnp.sum(cen * cen, axis=1, keepdims=True)
        inv_std = lax.rsqrt(sq * (1.0 / D) + 1e-06)
        for t in range(8):
            gain = gain_ref[t]
            normed = ((xg[t].astype(F32) - mean) * inv_std * gain).astype(BF16)
            g0 = gain.astype(BF16).astype(F32)
            g1 = (gain - g0).astype(BF16).astype(F32)
            g2 = (gain - g0 - g1).astype(BF16).astype(F32)
            gains = jnp.concatenate([g0, g1, g2, jnp.zeros((13, W), F32)], axis=0).astype(BF16)
            for half in range(2):
                lanes = slice(half * SLAB, (half + 1) * SLAB)
                nb[2 * t + half, 0:ROWS] = normed[:, lanes]
                nb[2 * t + half, ROWS:] = gains[:, lanes]
        st["mean"], st["inv_std"] = mean, inv_std

    st = {}

    def cot_start():
        cot_d.extend(gather_start(cg, S_COT))

    def cot_pass():
        cot_f.extend(gather_pass(cg, S_COT, cot_d))

    def x_pass():
        xg_f.extend(gather_pass(xg, S_XG, xg_d))

    b_step(0)
    a_first()
    cot_start()
    tiles_sort()
    b_step(1)
    relay_step(0)
    tiles_second()
    tiles_z(8,7,9,6,10)
    b_step(2)
    tiles_z(5,11,4,12,3)
    relay_step(1)
    a_step(0)
    b_step(3)
    tiles_z(13,2,14,1,15)
    relay_step(2)
    a_step(1)
    b_step(4)
    cot_pass()
    relay_step(3)
    a_step(2)
    b_step(5)
    relay_step(4)
    a_step(3)
    tiles_last()
    tiles_after()
    b_step(6)
    relay_step(5)
    a_step(4)
    b_step(7)
    grads_ready()
    relay_step(6)
    a_step(5)
    x_pass()
    b_step(8)
    norm()
    relay_step(7)
    a_step(6)
    project_qkv(0)
    project_qkv(1)
    relay_step(8)
    project_qkv(2)
    a_step(7)
    project_qkv(3)
    project_qkv(4)
    a_step(8)
    project_qkv(5)
    project_qkv(6)
    for j in range(9):
        project_grad(j)
    project_qkv(7)
    project_qkv(8)
    live, live_row, mean, inv_std = st["live"], st["live_row"], st["mean"], st["inv_std"]

    half_rows = ROWS // 2
    row_img = lax.shift_right_logical(
        lax.broadcasted_iota(jnp.int32, (half_rows, half_rows), 0), 3
    )
    col_img = lax.shift_right_logical(
        lax.broadcasted_iota(jnp.int32, (half_rows, half_rows), 1), 3
    )
    same = row_img == col_img
    scale = HD ** (-0.5)
    blocks = [
        (slice(r * half_rows, (r + 1) * half_rows), slice(h * HD, (h + 1) * HD))
        for r in range(2) for h in range(3)
    ]
    qkv = [[acc[i, rs, cols].astype(BF16) for i in range(3)] for rs, cols in blocks]
    ag = [acc[3, rs, cols].astype(BF16) for rs, cols in blocks]
    ok = [same & (live_row[:, rs] > 0.5) for rs, _ in blocks]
    sc = [jnp.where(m, dot(q, k, NT) * scale, -1e30) for m, (q, k, v) in zip(ok, qkv)]
    dprobs = [dot(a, v, NT) for a, (q, k, v) in zip(ag, qkv)]
    ex = [jnp.exp(a - jnp.max(a, axis=1, keepdims=True)) for a in sc]
    probs = [(a / jnp.sum(a, axis=1, keepdims=True)).astype(BF16) for a in ex]
    attn = [dot(p, v).astype(BF16) for p, (q, k, v) in zip(probs, qkv)]
    probs32 = [p.astype(F32) for p in probs]
    inner = [jnp.sum(d * p, axis=1, keepdims=True) for d, p in zip(dprobs, probs32)]
    sg = [(p * (d - n) * scale).astype(BF16) for p, d, n in zip(probs32, dprobs, inner)]
    vg = [dot(p, a, TN).astype(BF16) for p, a in zip(probs, ag)]
    qg = [dot(a, k).astype(BF16) for a, (q, k, v) in zip(sg, qkv)]
    kg = [dot(a, q, TN).astype(BF16) for a, (q, k, v) in zip(sg, qkv)]

    def whole(parts):
        return jnp.concatenate(
            [jnp.concatenate(parts[r * 3 : r * 3 + 3], axis=1) for r in range(2)], axis=0
        )

    grads = [whole(g) for g in (qg, kg, vg)]

    sib_nd, rs_n, sc_d = [], {}, []

    def partial(n):
        for t in range(8):
            rows = slice(t * W + n * 128, t * W + n * 128 + 128)
            p = dot(grads[0], wbuf[0, rows], NT)
            p = p + dot(grads[1], wbuf[1, rows], NT) + dot(grads[2], wbuf[2, rows], NT)
            part_n[t % 2, n, t // 2] = p.astype(BF16)
        sib_nd.append(copy(part_n.at[oc, n], sib_n.at[n], S_NS + n, (dp, tens(0, oc))))

    def fold(n):
        sib_nd[n].wait_recv()
        for k in (2, 1, 3):
            xx = lax.rem(x + k, NX)
            q_n[n, xx] = (part_n[c, n, xx].astype(F32) + sib_n[n, xx].astype(F32)).astype(BF16)
            rs_n[n, k] = copy(
                q_n.at[n, xx], rx_n.at[n, k - 1], S_NX + n * 3 + k - 1, (dp, tens(k, c))
            )

    def row_sums():
        s1, s2 = [], []
        for r in range(2):
            rs = slice(r * half_rows, (r + 1) * half_rows)
            a1s = jnp.zeros((half_rows, HD), F32)
            a2s = jnp.zeros((half_rows, HD), F32)
            for h in range(3):
                cols = slice(h * HD, (h + 1) * HD)
                for i, g in enumerate((qg, kg, vg)):
                    g32 = g[r * 3 + h].astype(F32)
                    a1s = a1s + g32 * jnp.sum(acc[i, ROWS:, cols], axis=0, keepdims=True)
                    a2s = a2s + g32 * acc[i, rs, cols]
            s1.append(jnp.sum(a1s, axis=1, keepdims=True))
            s2.append(jnp.sum(a2s, axis=1, keepdims=True))
        s1r = jnp.sum(jnp.where(eye, jnp.concatenate(s1, axis=0), 0.0), axis=0, keepdims=True)
        s2r = jnp.sum(jnp.where(eye, jnp.concatenate(s2, axis=0), 0.0), axis=0, keepdims=True)
        scal[tn] = jnp.concatenate([s1r, s2r, jnp.zeros((6, ROWS), F32)], axis=0)
        own_s = scal.at[tn]
        sc_d.extend([copy(own_s, own_s, S_SC + k - 1, (dp, tens(k, c))) for k in (1, 2, 3)])
        sc_d.extend([copy(own_s, own_s, S_SC + 3 + k, (dp, tens(k, oc))) for k in range(4)])

    partial(0)
    row_sums()
    partial(1)
    fold(0)
    partial(2)
    fold(1)
    fold(2)
    local = xg[tn].astype(F32)
    unit = (local - mean) * inv_std
    for d in sc_d:
        d.wait_recv()
    sums = scal[0]
    for t in range(1, 8):
        sums = sums + scal[t]
    mean1 = jnp.sum(jnp.where(eye, sums[0:1, :], 0.0), axis=1, keepdims=True) * (1.0 / D)
    mean2 = jnp.sum(jnp.where(eye, sums[1:2, :], 0.0), axis=1, keepdims=True) * (1.0 / D)

    r1, r2, rs_o = {}, {}, {}

    def return_z(n):
        lanes = slice(n * 128, n * 128 + 128)
        ng = part_n[c, n, x].astype(F32) + sib_n[n, x].astype(F32)
        for k in (1, 2, 3):
            rs_n[n, k].wait_recv()
            ng = ng + rx_n[n, k - 1].astype(F32)
        back = inv_std * (ng * gain_ref[tn][:, lanes] - mean1 - unit[:, lanes] * mean2)
        moved = jnp.where(live, cot_ref[:, lanes].astype(F32) + back, 0.0).astype(BF16)
        ret1[n] = dot(pick_t[...], moved).astype(BF16).reshape(NZ, 32, 128)
        for k in (8, 7, 9, 6, 10, 5, 11, 4, 12, 3, 13, 2, 14, 1, 15):
            p = lax.rem(z + k, NZ)
            r1[n, k] = copy(ret1.at[n, p], got1.at[n, z], S_R1 + n * 15 + k - 1, (at(k), tn))
        got1[n, z] = ret1[n, z]

    def return_y(n):
        for k in range(1, NZ):
            r1[n, k].wait_recv()
        tiles = got1[n].astype(F32)
        for q in range(NY):
            ret2[n, q] = jnp.concatenate(
                [tiles[s, q * 8 : q * 8 + 8, :] for s in range(NZ)], axis=0
            ).astype(BF16)
        for k in (1, 2, 3):
            p = lax.rem(y + k, NY)
            r2[n, k] = copy(ret2.at[n, p], got2.at[n, y], S_R2 + n * 3 + k - 1, (at(0, k), tn))
        got2[n, y] = ret2[n, y]

    def return_last(n):
        for k in (1, 2, 3):
            r2[n, k].wait_recv()
        pg_ref[:, n * 128 : n * 128 + 128] = dot(
            pack_t[...], got2[n].reshape(512, 128)
        ).astype(BF16)

    return_z(0)
    attn_all = whole(attn)
    for t in range(8):
        part_o[t % 2, t // 2] = dot(attn_all, wbuf[3, t * W : t * W + W], NT).astype(BF16)
    sib_od = copy(part_o.at[oc], sib_o, S_OS, (dp, tens(0, oc)))
    return_z(1)
    return_z(2)
    sib_od.wait_recv()
    for k in (2, 1, 3):
        xx = lax.rem(x + k, NX)
        q_o[xx] = (part_o[c, xx].astype(F32) + sib_o[xx].astype(F32)).astype(BF16)
        rs_o[k] = copy(q_o.at[xx], rx_o.at[k - 1], S_OX + k - 1, (dp, tens(k, c)))
    return_y(0)
    return_y(1)
    branch = part_o[c, x].astype(F32) + sib_o[x].astype(F32)
    for k in (1, 2, 3):
        rs_o[k].wait_recv()
        branch = branch + rx_o[k - 1].astype(F32)
    mixed_ref[...] = jnp.where(live, local + branch, 0.0).astype(BF16)
    return_last(0)
    return_y(2)
    return_last(1)
    return_last(2)
    for d in pending:
        d.wait_send()


def per_device(patches, counts, target, ln_gain, w_qkv, w_out, cotangent):
    images, slot_len, width = patches.shape
    vm = pl.BlockSpec(memory_space=pltpu.VMEM)
    b = lambda *s: pltpu.VMEM(s, BF16)
    f = lambda *s: pltpu.VMEM(s, F32)
    scratch = [
        b(ROWS, W), b(ROWS, W), f(8, 1, W),
        b(4, D, W), b(8, ROWS, W), b(8, ROWS, W), b(NZ, ROWS + 16, SLAB), b(NZ, ROWS, SLAB),
        b(NY, 128, W), b(NY, 128, W), b(NZ, 32, W), b(NZ, 32, W),
        f(NY, 1, 128), f(NY, 1, 128), f(NZ, NY, 1, 128),
        b(ROWS, 512), b(512, ROWS), b(ROWS, 512), f(4, ROWS + 16, W),
        b(2, 3, 4, ROWS, 128), b(2, 4, ROWS, W), b(3, 4, ROWS, 128), b(4, ROWS, W),
        b(3, 4, ROWS, 128), b(4, ROWS, W), b(3, 3, ROWS, 128), b(3, ROWS, W), f(8, 8, ROWS),
        b(3, NZ, 32, 128), b(3, NZ, 32, 128), b(3, NY, 128, 128), b(3, NY, 128, 128),
        pltpu.SemaphoreType.DMA((N_SEM,)), pltpu.SemaphoreType.DMA((N_SEM,)),
        pltpu.SemaphoreType.DMA((6,)),
    ]
    mixed, grad = pl.pallas_call(
        block_kernel,
        out_shape=[jax.ShapeDtypeStruct((ROWS, W), BF16)] * 2,
        in_specs=[vm] * 2 + [pl.BlockSpec(memory_space=pl.ANY)] * 5,
        out_specs=[vm] * 2,
        scratch_shapes=scratch,
        compiler_params=pltpu.CompilerParams(
            collective_id=0, has_side_effects=True, vmem_limit_bytes=56 << 20
        ),
        name="attention_block",
    )(
        target.reshape(1, images), counts.reshape(1, images), patches.reshape(ROWS, width),
        cotangent.reshape(ROWS, width), ln_gain.reshape(8, 1, W), w_qkv, w_out.T,
    )
    return mixed.reshape(patches.shape), grad.reshape(patches.shape)


def solution(mesh):
    in_specs = (
        P("dp", None, "tensor"), P("dp"), P("dp"), P(), P(None, "dp", "tensor"),
        P("tensor", "dp"), P("dp", None, "tensor"),
    )
    out_specs = (P("dp", None, "tensor"), P("dp", None, "tensor"))
    return jax.shard_map(
        per_device, mesh=mesh, in_specs=in_specs, out_specs=out_specs, check_vma=False
    )
```

```python
import jax
import jax.numpy as jnp
from jax import lax
from jax.experimental import pallas as pl
from jax.experimental.pallas import tpu as pltpu
from jax.sharding import PartitionSpec as P

HD = 128
D = 3072
NZ, NY, NX = 16, 4, 4
ROWS = 256
W = 384
SHARD = 48
SLAB = 192
F32 = jnp.float32
BF16 = jnp.bfloat16
NT = (((1,), (1,)), ((), ()))
TN = (((0,), (0,)), ((), ()))
S_COT = 0
S_XG = 7
S_A1 = 14
S_M1 = 17
S_A2 = 20
S_M2 = 35
S_AY = 50
S_AZR = 53
S_AZL = 60
S_BZR = 68
S_BZL = 76
S_BYR = 83
S_BYL = 99
S_BREL = 115
S_NS = 131
S_NX = 134
S_OS = 143
S_OX = 144
S_SC = 147
S_R1 = 154
S_R2 = 199
N_SEM = 208


def dot(a, b, dims=(((1,), (0,)), ((), ()))):
    return lax.dot_general(a, b, dims, preferred_element_type=F32)


def block_kernel(
    target_ref, counts_ref, x_hbm, cot_hbm, gain_hbm, wqkv_hbm, wout_hbm, mixed_ref, pg_ref,
    x_ref, cot_ref, gain_ref, wbuf, xg, cg, nb, gb, send, mid, mid2, recv, msend, mrecv, mall,
    pick, pick_t, pack_t, acc, part_n, part_o, sib_n, sib_o, q_n, q_o, rx_n, rx_o, scal,
    ret1, got1, ret2, got2, ssem, rsem, lsem,
):
    dp = lax.axis_index("dp")
    tn = lax.axis_index("tensor")
    z, y = lax.div(dp, NY), lax.rem(dp, NY)
    x, c = lax.div(tn, 2), lax.rem(tn, 2)
    oc = 1 - c

    def at(dz=0, dy=0):
        return lax.rem(z + dz + NZ, NZ) * NY + lax.rem(y + dy + NY, NY)

    def tens(dx, core):
        return lax.rem(x + dx, NX) * 2 + core

    def rows_of(p):
        return pl.ds(pl.multiple_of(p * SHARD, SHARD), SHARD)

    def slab(zz):
        return pl.ds(pl.multiple_of(zz * SLAB, SLAB), SLAB)

    barrier = pltpu.get_barrier_semaphore()
    peers = [(at(k, 0), tn) for k in range(1, NZ)]
    peers += [(at(0, k), tn) for k in range(1, NY)]
    peers += [(dp, tens(k, c)) for k in range(1, NX)]
    peers += [(dp, tens(k, oc)) for k in range(NX)]
    for peer in peers:
        pl.semaphore_signal(barrier, inc=1, device_id=peer, device_id_type=pl.DeviceIdType.MESH)
    loads = []
    for i, (a, b) in enumerate((
        (wqkv_hbm, wbuf.at[pl.ds(0, 3), rows_of(dp)]), (wout_hbm, wbuf.at[3, rows_of(dp)]),
        (cot_hbm, cg.at[tn]), (x_hbm, x_ref), (cot_hbm, cot_ref), (gain_hbm, gain_ref),
    )):
        loads.append(pltpu.make_async_copy(a, b, lsem.at[i]))
        loads[-1].start()

    pending = []

    def copy(src, dst, sem, to):
        desc = pltpu.make_async_remote_copy(
            src_ref=src, dst_ref=dst, send_sem=ssem.at[sem], recv_sem=rsem.at[sem],
            device_id=to, device_id_type=pl.DeviceIdType.MESH,
        )
        desc.start()
        pending.append(desc)
        return desc

    eye = lax.broadcasted_iota(jnp.int32, (ROWS, ROWS), 0) == lax.broadcasted_iota(
        jnp.int32, (ROWS, ROWS), 1
    )
    st = {}
    m1, a1 = [], []

    def tiles_sort():
        spread = (
            lax.shift_right_logical(lax.broadcasted_iota(jnp.int32, (32, ROWS), 1), 3)
            == lax.broadcasted_iota(jnp.int32, (32, ROWS), 0)
        ).astype(BF16)
        pair = jnp.concatenate(
            [target_ref[...].astype(F32), counts_ref[...].astype(F32), jnp.zeros((14, 32), F32)],
            axis=0,
        ).astype(BF16)
        pair = dot(pair, spread).astype(jnp.int32)
        lane = lax.broadcasted_iota(jnp.int32, (1, ROWS), 1)
        row = lax.bitwise_and(lane, 7)
        to = pair[0:1, :]
        dest = lax.bitwise_and(to, 3) * 128 + lax.shift_right_logical(to, 2) * 8 + row
        slot = jnp.where(row < pair[1:2, :], lane, -1)
        pack = (lax.broadcasted_iota(jnp.int32, (512, ROWS), 0) == dest).astype(BF16)
        send[...] = dot(pack, x_ref[...]).astype(BF16).reshape(NY, 128, W)
        a_meta = jnp.where(
            lax.broadcasted_iota(jnp.int32, (16, ROWS), 0) == lax.shift_right_logical(dest, 7),
            slot + 1, 0,
        ).astype(F32).astype(BF16)
        b_meta = (
            lax.broadcasted_iota(jnp.int32, (128, ROWS), 0) == lax.bitwise_and(dest, 127)
        ).astype(BF16)
        meta_rows = dot(a_meta, b_meta, NT)
        for k in range(NY):
            msend[k] = meta_rows[k : k + 1, :]
        mid[y] = send[y]
        mrecv[y] = msend[y]
        st["dest"] = dest

    def tiles_first():
        for k in (1, 2, 3):
            p = lax.rem(y + k, NY)
            m1.append(copy(msend.at[p], mrecv.at[y], S_M1 + k - 1, (at(0, k), tn)))
            a1.append(copy(send.at[p], mid.at[y], S_A1 + k - 1, (at(0, k), tn)))

    def tiles_order():
        pack = lax.broadcasted_iota(jnp.int32, (512, ROWS), 0) == st["dest"]
        pack_t[...] = dot(eye.astype(BF16), pack.astype(BF16), NT).astype(BF16)

    for d in loads:
        d.wait()
    pl.semaphore_wait(barrier, len(peers))

    def b_zr(j):
        r = wbuf.at[pl.ds(0, 3), rows_of(at(-j))]
        return copy(r, r, S_BZR + j, (at(1), tn))

    def b_zl(j):
        r = wbuf.at[pl.ds(0, 3), rows_of(at(j))]
        return copy(r, r, S_BZL + j, (at(-1), tn))

    def b_y(d):
        r = wbuf.at[pl.ds(0, 3), rows_of(at(d))]
        return copy(r, r, S_BYR + d, (at(0, 1), tn)), copy(r, r, S_BYL + d, (at(0, -1), tn))

    def b_relay(d, up):
        r = wbuf.at[pl.ds(0, 3), rows_of(at(d, -1 if up else 1))]
        return copy(r, r, S_BREL + d, (at(0, 1 if up else -1), tn))

    def a_zr(j):
        r = wbuf.at[3, slab(lax.rem(z - j + NZ, NZ))]
        return copy(r, r, S_AZR + j, (at(1), tn))

    def a_zl(j):
        r = wbuf.at[3, slab(lax.rem(z + j, NZ))]
        return copy(r, r, S_AZL + j, (at(-1), tn))

    zr, zl, yy, rel, azr, azl = {}, {}, {}, {}, {}, {}
    a_y, a2, m2, cot_d, cot_f, xg_d, xg_f = [], [], [], [], [], [], []

    def tiles_second():
        for d in a1 + m1:
            d.wait_recv()
        tiles = mid[...].astype(F32)
        for q in range(NZ):
            mid2[q] = jnp.concatenate(
                [tiles[s, q * 8 : q * 8 + 8, :] for s in range(NY)], axis=0
            ).astype(BF16)
        recv[z] = mid2[z]
        mall[z] = mrecv[...]

    def tiles_z(*ks):
        for k in ks:
            p = lax.rem(z + k, NZ)
            m2.append(copy(mrecv, mall.at[z], S_M2 + k - 1, (at(k), tn)))
            a2.append(copy(mid2.at[p], recv.at[z], S_A2 + k - 1, (at(k), tn)))

    def tiles_last():
        for d in a2 + m2:
            d.wait_recv()
        lane = lax.broadcasted_iota(jnp.int32, (128, 512), 1)
        sel = (
            lax.broadcasted_iota(jnp.int32, (128, 512), 0) == z * 8 + lax.bitwise_and(lane, 7)
        ).astype(BF16)
        mine = (
            lax.broadcasted_iota(jnp.int32, (64, 512), 0)
            == lax.shift_right_logical(lax.broadcasted_iota(jnp.int32, (64, 512), 1), 3)
        )
        rows = jnp.concatenate([mall[q, s] for q in range(NZ) for s in range(NY)], axis=0)
        where_to = jnp.sum(
            jnp.where(mine, dot(rows.astype(BF16), sel), 0.0), axis=0, keepdims=True
        ).astype(jnp.int32) - 1
        picked = (lax.broadcasted_iota(jnp.int32, (ROWS, 512), 0) == where_to).astype(BF16)
        pick[...] = picked
        xg[tn] = dot(picked, recv[...].reshape(512, W)).astype(BF16)
        xg_d.extend(gather_start(xg, S_XG))

    def tiles_after():
        eye512 = lax.broadcasted_iota(jnp.int32, (512, 512), 0) == lax.broadcasted_iota(
            jnp.int32, (512, 512), 1
        )
        pick_t[...] = dot(eye512.astype(BF16), pick[...], NT).astype(BF16)
        live_col = jnp.sum(pick[...].astype(F32), axis=1, keepdims=True)
        st["live_row"] = jnp.sum(jnp.where(eye, live_col, 0.0), axis=0, keepdims=True)
        st["live"] = live_col > 0.5

    def gather_start(buf, base):
        own = buf.at[tn]
        sib = copy(own, own, base, (dp, tens(0, oc)))
        return [sib] + [copy(own, own, base + k, (dp, tens(k, c))) for k in (1, 2, 3)]

    def gather_pass(buf, base, ds):
        out = []
        for k in (1, 2, 3):
            ds[k].wait_recv()
            r = buf.at[tens(NX - k, c)]
            out.append(copy(r, r, base + 3 + k, (dp, tens(0, oc))))
        return out

    def a_first():
        for k in (1, 2, 3):
            r = wbuf.at[3, rows_of(dp)]
            a_y.append(copy(r, r, S_AY + k - 1, (at(0, k), tn)))

    def b_step(j):
        if j == 0:
            zr[0], zl[0] = b_zr(0), b_zl(0)
            yy[0] = b_y(0)
            return
        zr[j - 1].wait_recv()
        if j < 8:
            zr[j] = b_zr(j)
        yy[NZ - j] = b_y(NZ - j)
        if j < 8:
            zl[j - 1].wait_recv()
            if j < 7:
                zl[j] = b_zl(j)
            yy[j] = b_y(j)

    def relay_step(j):
        if j > 0:
            d = NZ - j
            yy[d][0].wait_recv()
            rel[d] = b_relay(d, True)
        if j < 8:
            yy[j][1].wait_recv()
            rel[j] = b_relay(j, False)

    def a_step(j):
        if j == 0:
            for d in a_y:
                d.wait_recv()
        else:
            azl[j - 1].wait_recv()
            if j < 8:
                azr[j - 1].wait_recv()
        if j < 8:
            azl[j] = a_zl(j)
        if j < 7:
            azr[j] = a_zr(j)

    def b_done(j):
        d = (NZ - j) % NZ
        if j > 0:
            yy[d][1].wait_recv()
            rel[d].wait_recv()
        if j < 8:
            yy[j][0].wait_recv()
            rel[j].wait_recv()

    def project_qkv(j):
        b_done(j)
        for zz in {0: (z,), 8: (lax.rem(z + 8, NZ),)}.get(
            j, (lax.rem(z + j, NZ), lax.rem(z - j + NZ, NZ))
        ):
            rows = nb[zz]
            for i in range(3):
                p = dot(rows, wbuf[i, slab(zz)])
                acc[i] = p if j == 0 else acc[i] + p

    def project_grad(j):
        for zz in {0: (z,), 8: (lax.rem(z + 8, NZ),)}.get(
            j, (lax.rem(z + j, NZ), lax.rem(z - j + NZ, NZ))
        ):
            p = dot(gb[zz], wbuf[3, slab(zz)])
            acc[3, 0:ROWS] = p if j == 0 else acc[3, 0:ROWS] + p

    def grads_ready():
        cot_d[0].wait_recv()
        for d in cot_f:
            d.wait_recv()
        for t in range(8):
            g = jnp.where(st["live"], cg[t], jnp.zeros((), BF16))
            gb[2 * t] = g[:, :SLAB]
            gb[2 * t + 1] = g[:, SLAB:]

    def norm():
        xg_d[0].wait_recv()
        for d in xg_f:
            d.wait_recv()
        total = jnp.zeros((ROWS, 1), F32)
        for t in range(8):
            total = total + jnp.sum(xg[t].astype(F32), axis=1, keepdims=True)
        mean = total * (1.0 / D)
        sq = jnp.zeros((ROWS, 1), F32)
        for t in range(8):
            cen = xg[t].astype(F32) - mean
            sq = sq + jnp.sum(cen * cen, axis=1, keepdims=True)
        inv_std = lax.rsqrt(sq * (1.0 / D) + 1e-06)
        for t in range(8):
            gain = gain_ref[t]
            normed = ((xg[t].astype(F32) - mean) * inv_std * gain).astype(BF16)
            g0 = gain.astype(BF16).astype(F32)
            g1 = (gain - g0).astype(BF16).astype(F32)
            g2 = (gain - g0 - g1).astype(BF16).astype(F32)
            gains = jnp.concatenate([g0, g1, g2, jnp.zeros((13, W), F32)], axis=0).astype(BF16)
            for half in range(2):
                lanes = slice(half * SLAB, (half + 1) * SLAB)
                nb[2 * t + half, 0:ROWS] = normed[:, lanes]
                nb[2 * t + half, ROWS:] = gains[:, lanes]
        st["mean"], st["inv_std"] = mean, inv_std

    def cot_start():
        cot_d.extend(gather_start(cg, S_COT))

    def cot_pass():
        cot_f.extend(gather_pass(cg, S_COT, cot_d))

    def x_pass():
        xg_f.extend(gather_pass(xg, S_XG, xg_d))

    b_step(0)
    a_first()
    cot_start()
    tiles_sort()
    tiles_first()
    b_step(1)
    a_step(0)
    relay_step(0)
    tiles_second()
    tiles_z(1,15,2,14)
    b_step(2)
    a_step(1)
    tiles_z(3,13,4,12)
    relay_step(1)
    b_step(3)
    a_step(2)
    tiles_z(5,11,6,10)
    relay_step(2)
    b_step(4)
    a_step(3)
    tiles_z(7,9,8)
    cot_pass()
    relay_step(3)
    b_step(5)
    a_step(4)
    relay_step(4)
    tiles_last()
    b_step(6)
    a_step(5)
    tiles_after()
    tiles_order()
    relay_step(5)
    b_step(7)
    a_step(6)
    grads_ready()
    relay_step(6)
    x_pass()
    b_step(8)
    a_step(7)
    relay_step(7)
    norm()
    relay_step(8)
    a_step(8)
    project_qkv(0)
    project_qkv(1)
    project_qkv(2)
    project_qkv(3)
    project_qkv(4)
    project_qkv(5)
    project_qkv(6)
    for j in range(9):
        project_grad(j)
    project_qkv(7)
    project_qkv(8)
    live, live_row, mean, inv_std = st["live"], st["live_row"], st["mean"], st["inv_std"]

    half_rows = ROWS // 2
    row_img = lax.shift_right_logical(
        lax.broadcasted_iota(jnp.int32, (half_rows, half_rows), 0), 3
    )
    col_img = lax.shift_right_logical(
        lax.broadcasted_iota(jnp.int32, (half_rows, half_rows), 1), 3
    )
    same = row_img == col_img
    scale = HD ** (-0.5)
    blocks = [
        (slice(r * half_rows, (r + 1) * half_rows), slice(h * HD, (h + 1) * HD))
        for r in range(2) for h in range(3)
    ]
    qkv = [[acc[i, rs, cols].astype(BF16) for i in range(3)] for rs, cols in blocks]
    ag = [acc[3, rs, cols].astype(BF16) for rs, cols in blocks]
    ok = [same & (live_row[:, rs] > 0.5) for rs, _ in blocks]
    sc = [jnp.where(m, dot(q, k, NT) * scale, -1e30) for m, (q, k, v) in zip(ok, qkv)]
    dprobs = [dot(a, v, NT) for a, (q, k, v) in zip(ag, qkv)]
    ex = [jnp.exp(a - jnp.max(a, axis=1, keepdims=True)) for a in sc]
    probs = [(a / jnp.sum(a, axis=1, keepdims=True)).astype(BF16) for a in ex]
    attn = [dot(p, v).astype(BF16) for p, (q, k, v) in zip(probs, qkv)]
    probs32 = [p.astype(F32) for p in probs]
    inner = [jnp.sum(d * p, axis=1, keepdims=True) for d, p in zip(dprobs, probs32)]
    sg = [(p * (d - n) * scale).astype(BF16) for p, d, n in zip(probs32, dprobs, inner)]
    vg = [dot(p, a, TN).astype(BF16) for p, a in zip(probs, ag)]
    qg = [dot(a, k).astype(BF16) for a, (q, k, v) in zip(sg, qkv)]
    kg = [dot(a, q, TN).astype(BF16) for a, (q, k, v) in zip(sg, qkv)]

    def whole(parts):
        return jnp.concatenate(
            [jnp.concatenate(parts[r * 3 : r * 3 + 3], axis=1) for r in range(2)], axis=0
        )

    grads = [whole(g) for g in (qg, kg, vg)]

    sib_nd, rs_n, sc_d = [], {}, []

    def partial(n):
        for t in range(8):
            rows = slice(t * W + n * 128, t * W + n * 128 + 128)
            p = dot(grads[0], wbuf[0, rows], NT)
            p = p + dot(grads[1], wbuf[1, rows], NT) + dot(grads[2], wbuf[2, rows], NT)
            part_n[t % 2, n, t // 2] = p.astype(BF16)
        if n == 0:
            row_sums()
        sib_nd.append(copy(part_n.at[oc, n], sib_n.at[n], S_NS + n, (dp, tens(0, oc))))

    def fold(n):
        sib_nd[n].wait_recv()
        for k in (2, 1, 3):
            xx = lax.rem(x + k, NX)
            q_n[n, xx] = (part_n[c, n, xx].astype(F32) + sib_n[n, xx].astype(F32)).astype(BF16)
            rs_n[n, k] = copy(
                q_n.at[n, xx], rx_n.at[n, k - 1], S_NX + n * 3 + k - 1, (dp, tens(k, c))
            )

    def row_sums():
        s1, s2 = [], []
        for r in range(2):
            rs = slice(r * half_rows, (r + 1) * half_rows)
            a1s = jnp.zeros((half_rows, HD), F32)
            a2s = jnp.zeros((half_rows, HD), F32)
            for h in range(3):
                cols = slice(h * HD, (h + 1) * HD)
                for i, g in enumerate((qg, kg, vg)):
                    g32 = g[r * 3 + h].astype(F32)
                    a1s = a1s + g32 * jnp.sum(acc[i, ROWS:, cols], axis=0, keepdims=True)
                    a2s = a2s + g32 * acc[i, rs, cols]
            s1.append(jnp.sum(a1s, axis=1, keepdims=True))
            s2.append(jnp.sum(a2s, axis=1, keepdims=True))
        s1r = jnp.sum(jnp.where(eye, jnp.concatenate(s1, axis=0), 0.0), axis=0, keepdims=True)
        s2r = jnp.sum(jnp.where(eye, jnp.concatenate(s2, axis=0), 0.0), axis=0, keepdims=True)
        scal[tn] = jnp.concatenate([s1r, s2r, jnp.zeros((6, ROWS), F32)], axis=0)

    def send_sums():
        own_s = scal.at[tn]
        sc_d.extend([copy(own_s, own_s, S_SC + k - 1, (dp, tens(k, c))) for k in (1, 2, 3)])
        sc_d.extend([copy(own_s, own_s, S_SC + 3 + k, (dp, tens(k, oc))) for k in range(4)])

    partial(0)
    send_sums()
    partial(1)
    fold(0)
    partial(2)
    fold(1)
    fold(2)
    local = xg[tn].astype(F32)
    unit = (local - mean) * inv_std
    for d in sc_d:
        d.wait_recv()
    sums = scal[0]
    for t in range(1, 8):
        sums = sums + scal[t]
    mean1 = jnp.sum(jnp.where(eye, sums[0:1, :], 0.0), axis=1, keepdims=True) * (1.0 / D)
    mean2 = jnp.sum(jnp.where(eye, sums[1:2, :], 0.0), axis=1, keepdims=True) * (1.0 / D)

    r1, r2, rs_o = {}, {}, {}

    def return_z(n):
        lanes = slice(n * 128, n * 128 + 128)
        ng = part_n[c, n, x].astype(F32) + sib_n[n, x].astype(F32)
        for k in (1, 2, 3):
            rs_n[n, k].wait_recv()
            ng = ng + rx_n[n, k - 1].astype(F32)
        back = inv_std * (ng * gain_ref[tn][:, lanes] - mean1 - unit[:, lanes] * mean2)
        moved = jnp.where(live, cot_ref[:, lanes].astype(F32) + back, 0.0).astype(BF16)
        ret1[n] = dot(pick_t[...], moved).astype(BF16).reshape(NZ, 32, 128)
        for k in (8, 7, 9, 6, 10, 5, 11, 4, 12, 3, 13, 2, 14, 1, 15):
            p = lax.rem(z + k, NZ)
            r1[n, k] = copy(ret1.at[n, p], got1.at[n, z], S_R1 + n * 15 + k - 1, (at(k), tn))
        got1[n, z] = ret1[n, z]

    def return_y(n):
        for k in range(1, NZ):
            r1[n, k].wait_recv()
        tiles = got1[n].astype(F32)
        for q in range(NY):
            ret2[n, q] = jnp.concatenate(
                [tiles[s, q * 8 : q * 8 + 8, :] for s in range(NZ)], axis=0
            ).astype(BF16)
        for k in (1, 2, 3):
            p = lax.rem(y + k, NY)
            r2[n, k] = copy(ret2.at[n, p], got2.at[n, y], S_R2 + n * 3 + k - 1, (at(0, k), tn))
        got2[n, y] = ret2[n, y]

    def return_last(n):
        for k in (1, 2, 3):
            r2[n, k].wait_recv()
        pg_ref[:, n * 128 : n * 128 + 128] = dot(
            pack_t[...], got2[n].reshape(512, 128)
        ).astype(BF16)

    return_z(0)
    attn_all = whole(attn)
    for t in range(8):
        part_o[t % 2, t // 2] = dot(attn_all, wbuf[3, t * W : t * W + W], NT).astype(BF16)
    sib_od = copy(part_o.at[oc], sib_o, S_OS, (dp, tens(0, oc)))
    return_z(1)
    return_z(2)
    sib_od.wait_recv()
    for k in (2, 1, 3):
        xx = lax.rem(x + k, NX)
        q_o[xx] = (part_o[c, xx].astype(F32) + sib_o[xx].astype(F32)).astype(BF16)
        rs_o[k] = copy(q_o.at[xx], rx_o.at[k - 1], S_OX + k - 1, (dp, tens(k, c)))
    return_y(0)
    return_y(1)
    branch = part_o[c, x].astype(F32) + sib_o[x].astype(F32)
    for k in (1, 2, 3):
        rs_o[k].wait_recv()
        branch = branch + rx_o[k - 1].astype(F32)
    mixed_ref[...] = jnp.where(live, local + branch, 0.0).astype(BF16)
    return_last(0)
    return_y(2)
    return_last(1)
    return_last(2)
    for d in pending:
        d.wait_send()


def per_device(patches, counts, target, ln_gain, w_qkv, w_out, cotangent):
    images, slot_len, width = patches.shape
    vm = pl.BlockSpec(memory_space=pltpu.VMEM)
    b = lambda *s: pltpu.VMEM(s, BF16)
    f = lambda *s: pltpu.VMEM(s, F32)
    scratch = [
        b(ROWS, W), b(ROWS, W), f(8, 1, W),
        b(4, D, W), b(8, ROWS, W), b(8, ROWS, W), b(NZ, ROWS + 16, SLAB), b(NZ, ROWS, SLAB),
        b(NY, 128, W), b(NY, 128, W), b(NZ, 32, W), b(NZ, 32, W),
        f(NY, 1, 128), f(NY, 1, 128), f(NZ, NY, 1, 128),
        b(ROWS, 512), b(512, ROWS), b(ROWS, 512), f(4, ROWS + 16, W),
        b(2, 3, 4, ROWS, 128), b(2, 4, ROWS, W), b(3, 4, ROWS, 128), b(4, ROWS, W),
        b(3, 4, ROWS, 128), b(4, ROWS, W), b(3, 3, ROWS, 128), b(3, ROWS, W), f(8, 8, ROWS),
        b(3, NZ, 32, 128), b(3, NZ, 32, 128), b(3, NY, 128, 128), b(3, NY, 128, 128),
        pltpu.SemaphoreType.DMA((N_SEM,)), pltpu.SemaphoreType.DMA((N_SEM,)),
        pltpu.SemaphoreType.DMA((6,)),
    ]
    mixed, grad = pl.pallas_call(
        block_kernel,
        out_shape=[jax.ShapeDtypeStruct((ROWS, W), BF16)] * 2,
        in_specs=[vm] * 2 + [pl.BlockSpec(memory_space=pl.ANY)] * 5,
        out_specs=[vm] * 2,
        scratch_shapes=scratch,
        compiler_params=pltpu.CompilerParams(
            collective_id=0, has_side_effects=True, vmem_limit_bytes=56 << 20
        ),
        name="attention_block",
    )(
        target.reshape(1, images), counts.reshape(1, images), patches.reshape(ROWS, width),
        cotangent.reshape(ROWS, width), ln_gain.reshape(8, 1, W), w_qkv, w_out.T,
    )
    return mixed.reshape(patches.shape), grad.reshape(patches.shape)


def solution(mesh):
    in_specs = (
        P("dp", None, "tensor"), P("dp"), P("dp"), P(), P(None, "dp", "tensor"),
        P("tensor", "dp"), P("dp", None, "tensor"),
    )
    out_specs = (P("dp", None, "tensor"), P("dp", None, "tensor"))
    return jax.shard_map(
        per_device, mesh=mesh, in_specs=in_specs, out_specs=out_specs, check_vma=False
    )
```

```python
import jax
import jax.numpy as jnp
from jax import lax
from jax.experimental import pallas as pl
from jax.experimental.pallas import tpu as pltpu
from jax.sharding import PartitionSpec as P

HD = 128
D = 3072
NZ, NY, NX = 16, 4, 4
ROWS = 256
W = 384
SHARD = 48
SLAB = 192
F32 = jnp.float32
BF16 = jnp.bfloat16
NT = (((1,), (1,)), ((), ()))
TN = (((0,), (0,)), ((), ()))
S_COT = 0
S_XG = 7
S_A1 = 14
S_M1 = 17
S_A2 = 20
S_M2 = 35
S_AY = 50
S_AZR = 53
S_AZL = 60
S_BZR = 68
S_BZL = 76
S_BYR = 83
S_BYL = 99
S_BREL = 115
S_NS = 131
S_NX = 134
S_OS = 143
S_OX = 144
S_SC = 147
S_R1 = 154
S_R2 = 199
N_SEM = 208


def dot(a, b, dims=(((1,), (0,)), ((), ()))):
    return lax.dot_general(a, b, dims, preferred_element_type=F32)


def block_kernel(
    target_ref, counts_ref, x_hbm, cot_hbm, gain_hbm, wqkv_hbm, wout_hbm, mixed_ref, pg_ref,
    x_ref, cot_ref, gain_ref, wbuf, xg, cg, nb, gb, send, mid, mid2, recv, msend, mrecv, mall,
    pick, pick_t, pack_t, acc, part_n, part_o, sib_n, sib_o, q_n, q_o, rx_n, rx_o, scal,
    ret1, got1, ret2, got2, ssem, rsem, lsem,
):
    dp = lax.axis_index("dp")
    tn = lax.axis_index("tensor")
    z, y = lax.div(dp, NY), lax.rem(dp, NY)
    x, c = lax.div(tn, 2), lax.rem(tn, 2)
    oc = 1 - c

    def at(dz=0, dy=0):
        return lax.rem(z + dz + NZ, NZ) * NY + lax.rem(y + dy + NY, NY)

    def tens(dx, core):
        return lax.rem(x + dx, NX) * 2 + core

    def rows_of(p):
        return pl.ds(pl.multiple_of(p * SHARD, SHARD), SHARD)

    def slab(zz):
        return pl.ds(pl.multiple_of(zz * SLAB, SLAB), SLAB)

    barrier = pltpu.get_barrier_semaphore()
    peers = [(at(k, 0), tn) for k in range(1, NZ)]
    peers += [(at(0, k), tn) for k in range(1, NY)]
    peers += [(dp, tens(k, c)) for k in range(1, NX)]
    peers += [(dp, tens(k, oc)) for k in range(NX)]
    for peer in peers:
        pl.semaphore_signal(barrier, inc=1, device_id=peer, device_id_type=pl.DeviceIdType.MESH)
    loads = []
    for i, (a, b) in enumerate((
        (wqkv_hbm, wbuf.at[pl.ds(0, 3), rows_of(dp)]), (wout_hbm, wbuf.at[3, rows_of(dp)]),
        (cot_hbm, cg.at[tn]), (x_hbm, x_ref), (cot_hbm, cot_ref), (gain_hbm, gain_ref),
    )):
        loads.append(pltpu.make_async_copy(a, b, lsem.at[i]))
        loads[-1].start()

    pending = []

    def copy(src, dst, sem, to):
        desc = pltpu.make_async_remote_copy(
            src_ref=src, dst_ref=dst, send_sem=ssem.at[sem], recv_sem=rsem.at[sem],
            device_id=to, device_id_type=pl.DeviceIdType.MESH,
        )
        desc.start()
        pending.append(desc)
        return desc

    eye = lax.broadcasted_iota(jnp.int32, (ROWS, ROWS), 0) == lax.broadcasted_iota(
        jnp.int32, (ROWS, ROWS), 1
    )
    st = {}
    m1, a1 = [], []

    def tiles_sort():
        spread = (
            lax.shift_right_logical(lax.broadcasted_iota(jnp.int32, (32, ROWS), 1), 3)
            == lax.broadcasted_iota(jnp.int32, (32, ROWS), 0)
        ).astype(BF16)
        pair = jnp.concatenate(
            [target_ref[...].astype(F32), counts_ref[...].astype(F32), jnp.zeros((14, 32), F32)],
            axis=0,
        ).astype(BF16)
        pair = dot(pair, spread).astype(jnp.int32)
        lane = lax.broadcasted_iota(jnp.int32, (1, ROWS), 1)
        row = lax.bitwise_and(lane, 7)
        to = pair[0:1, :]
        dest = lax.bitwise_and(to, 3) * 128 + lax.shift_right_logical(to, 2) * 8 + row
        slot = jnp.where(row < pair[1:2, :], lane, -1)
        pack = (lax.broadcasted_iota(jnp.int32, (512, ROWS), 0) == dest).astype(BF16)
        send[...] = dot(pack, x_ref[...]).astype(BF16).reshape(NY, 128, W)
        a_meta = jnp.where(
            lax.broadcasted_iota(jnp.int32, (16, ROWS), 0) == lax.shift_right_logical(dest, 7),
            slot + 1, 0,
        ).astype(F32).astype(BF16)
        b_meta = (
            lax.broadcasted_iota(jnp.int32, (128, ROWS), 0) == lax.bitwise_and(dest, 127)
        ).astype(BF16)
        meta_rows = dot(a_meta, b_meta, NT)
        for k in range(NY):
            msend[k] = meta_rows[k : k + 1, :]
        mid[y] = send[y]
        mrecv[y] = msend[y]
        st["dest"] = dest

    def tiles_first():
        for k in (1, 2, 3):
            p = lax.rem(y + k, NY)
            m1.append(copy(msend.at[p], mrecv.at[y], S_M1 + k - 1, (at(0, k), tn)))
            a1.append(copy(send.at[p], mid.at[y], S_A1 + k - 1, (at(0, k), tn)))

    def tiles_order():
        pack = lax.broadcasted_iota(jnp.int32, (512, ROWS), 0) == st["dest"]
        pack_t[...] = dot(eye.astype(BF16), pack.astype(BF16), NT).astype(BF16)

    for d in loads:
        d.wait()
    pl.semaphore_wait(barrier, len(peers))

    def b_zr(j):
        r = wbuf.at[pl.ds(0, 3), rows_of(at(-j))]
        return copy(r, r, S_BZR + j, (at(1), tn))

    def b_zl(j):
        r = wbuf.at[pl.ds(0, 3), rows_of(at(j))]
        return copy(r, r, S_BZL + j, (at(-1), tn))

    def b_y(d):
        r = wbuf.at[pl.ds(0, 3), rows_of(at(d))]
        return copy(r, r, S_BYR + d, (at(0, 1), tn)), copy(r, r, S_BYL + d, (at(0, -1), tn))

    def b_relay(d, up):
        r = wbuf.at[pl.ds(0, 3), rows_of(at(d, -1 if up else 1))]
        return copy(r, r, S_BREL + d, (at(0, 1 if up else -1), tn))

    def a_zr(j):
        r = wbuf.at[3, slab(lax.rem(z - j + NZ, NZ))]
        return copy(r, r, S_AZR + j, (at(1), tn))

    def a_zl(j):
        r = wbuf.at[3, slab(lax.rem(z + j, NZ))]
        return copy(r, r, S_AZL + j, (at(-1), tn))

    zr, zl, yy, rel, azr, azl = {}, {}, {}, {}, {}, {}
    a_y, a2, m2, cot_d, cot_f, xg_d, xg_f = [], [], [], [], [], [], []

    def tiles_second():
        for d in a1 + m1:
            d.wait_recv()
        tiles = mid[...].astype(F32)
        for q in range(NZ):
            mid2[q] = jnp.concatenate(
                [tiles[s, q * 8 : q * 8 + 8, :] for s in range(NY)], axis=0
            ).astype(BF16)
        recv[z] = mid2[z]
        mall[z] = mrecv[...]

    def tiles_z(*ks):
        for k in ks:
            p = lax.rem(z + k, NZ)
            m2.append(copy(mrecv, mall.at[z], S_M2 + k - 1, (at(k), tn)))
            a2.append(copy(mid2.at[p], recv.at[z], S_A2 + k - 1, (at(k), tn)))

    def tiles_last():
        for d in a2 + m2:
            d.wait_recv()
        lane = lax.broadcasted_iota(jnp.int32, (128, 512), 1)
        sel = (
            lax.broadcasted_iota(jnp.int32, (128, 512), 0) == z * 8 + lax.bitwise_and(lane, 7)
        ).astype(BF16)
        mine = (
            lax.broadcasted_iota(jnp.int32, (64, 512), 0)
            == lax.shift_right_logical(lax.broadcasted_iota(jnp.int32, (64, 512), 1), 3)
        )
        rows = jnp.concatenate([mall[q, s] for q in range(NZ) for s in range(NY)], axis=0)
        where_to = jnp.sum(
            jnp.where(mine, dot(rows.astype(BF16), sel), 0.0), axis=0, keepdims=True
        ).astype(jnp.int32) - 1
        picked = (lax.broadcasted_iota(jnp.int32, (ROWS, 512), 0) == where_to).astype(BF16)
        pick[...] = picked
        xg[tn] = dot(picked, recv[...].reshape(512, W)).astype(BF16)
        xg_d.extend(gather_start(xg, S_XG))

    def tiles_after():
        eye512 = lax.broadcasted_iota(jnp.int32, (512, 512), 0) == lax.broadcasted_iota(
            jnp.int32, (512, 512), 1
        )
        pick_t[...] = dot(eye512.astype(BF16), pick[...], NT).astype(BF16)
        live_col = jnp.sum(pick[...].astype(F32), axis=1, keepdims=True)
        st["live_row"] = jnp.sum(jnp.where(eye, live_col, 0.0), axis=0, keepdims=True)
        st["live"] = live_col > 0.5

    def gather_start(buf, base):
        own = buf.at[tn]
        sib = copy(own, own, base, (dp, tens(0, oc)))
        return [sib] + [copy(own, own, base + k, (dp, tens(k, c))) for k in (1, 2, 3)]

    def gather_pass(buf, base, ds):
        out = []
        for k in (1, 2, 3):
            ds[k].wait_recv()
            r = buf.at[tens(NX - k, c)]
            out.append(copy(r, r, base + 3 + k, (dp, tens(0, oc))))
        return out

    def a_first():
        for k in (1, 2, 3):
            r = wbuf.at[3, rows_of(dp)]
            a_y.append(copy(r, r, S_AY + k - 1, (at(0, k), tn)))

    def b_step(j):
        if j == 0:
            zr[0], zl[0] = b_zr(0), b_zl(0)
            yy[0] = b_y(0)
            return
        zr[j - 1].wait_recv()
        if j < 8:
            zr[j] = b_zr(j)
        yy[NZ - j] = b_y(NZ - j)
        if j < 8:
            zl[j - 1].wait_recv()
            if j < 7:
                zl[j] = b_zl(j)
            yy[j] = b_y(j)

    def relay_step(j):
        if j > 0:
            d = NZ - j
            yy[d][0].wait_recv()
            rel[d] = b_relay(d, True)
        if j < 8:
            yy[j][1].wait_recv()
            rel[j] = b_relay(j, False)

    def a_step(j):
        if j == 0:
            for d in a_y:
                d.wait_recv()
        else:
            azl[j - 1].wait_recv()
            if j < 8:
                azr[j - 1].wait_recv()
        if j < 8:
            azl[j] = a_zl(j)
        if j < 7:
            azr[j] = a_zr(j)

    def b_done(j):
        d = (NZ - j) % NZ
        if j > 0:
            yy[d][1].wait_recv()
            rel[d].wait_recv()
        if j < 8:
            yy[j][0].wait_recv()
            rel[j].wait_recv()

    def project_qkv(j):
        b_done(j)
        for zz in {0: (z,), 8: (lax.rem(z + 8, NZ),)}.get(
            j, (lax.rem(z + j, NZ), lax.rem(z - j + NZ, NZ))
        ):
            rows = nb[zz]
            for i in range(3):
                p = dot(rows, wbuf[i, slab(zz)])
                acc[i] = p if j == 0 else acc[i] + p

    def project_grad(j):
        for zz in {0: (z,), 8: (lax.rem(z + 8, NZ),)}.get(
            j, (lax.rem(z + j, NZ), lax.rem(z - j + NZ, NZ))
        ):
            p = dot(gb[zz], wbuf[3, slab(zz)])
            acc[3, 0:ROWS] = p if j == 0 else acc[3, 0:ROWS] + p

    def grads_ready():
        cot_d[0].wait_recv()
        for d in cot_f:
            d.wait_recv()
        for t in range(8):
            g = jnp.where(st["live"], cg[t], jnp.zeros((), BF16))
            gb[2 * t] = g[:, :SLAB]
            gb[2 * t + 1] = g[:, SLAB:]

    def norm():
        xg_d[0].wait_recv()
        for d in xg_f:
            d.wait_recv()
        total = jnp.zeros((ROWS, 1), F32)
        for t in range(8):
            total = total + jnp.sum(xg[t].astype(F32), axis=1, keepdims=True)
        mean = total * (1.0 / D)
        sq = jnp.zeros((ROWS, 1), F32)
        for t in range(8):
            cen = xg[t].astype(F32) - mean
            sq = sq + jnp.sum(cen * cen, axis=1, keepdims=True)
        inv_std = lax.rsqrt(sq * (1.0 / D) + 1e-06)
        for t in range(8):
            gain = gain_ref[t]
            normed = ((xg[t].astype(F32) - mean) * inv_std * gain).astype(BF16)
            g0 = gain.astype(BF16).astype(F32)
            g1 = (gain - g0).astype(BF16).astype(F32)
            g2 = (gain - g0 - g1).astype(BF16).astype(F32)
            gains = jnp.concatenate([g0, g1, g2, jnp.zeros((13, W), F32)], axis=0).astype(BF16)
            for half in range(2):
                lanes = slice(half * SLAB, (half + 1) * SLAB)
                nb[2 * t + half, 0:ROWS] = normed[:, lanes]
                nb[2 * t + half, ROWS:] = gains[:, lanes]
        st["mean"], st["inv_std"] = mean, inv_std

    def cot_start():
        cot_d.extend(gather_start(cg, S_COT))

    def cot_pass():
        cot_f.extend(gather_pass(cg, S_COT, cot_d))

    def x_pass():
        xg_f.extend(gather_pass(xg, S_XG, xg_d))

    b_step(0)
    a_first()
    cot_start()
    tiles_sort()
    tiles_first()
    b_step(1)
    a_step(0)
    relay_step(0)
    b_step(2)
    a_step(1)
    tiles_second()
    tiles_z(1,15,2,14)
    tiles_z(3,13,4,12)
    relay_step(1)
    b_step(3)
    a_step(2)
    tiles_z(5,11,6,10)
    relay_step(2)
    b_step(4)
    a_step(3)
    tiles_z(7,9,8)
    cot_pass()
    relay_step(3)
    b_step(5)
    a_step(4)
    relay_step(4)
    tiles_last()
    b_step(6)
    a_step(5)
    tiles_after()
    tiles_order()
    relay_step(5)
    b_step(7)
    a_step(6)
    grads_ready()
    relay_step(6)
    x_pass()
    b_step(8)
    a_step(7)
    relay_step(7)
    norm()
    relay_step(8)
    a_step(8)
    project_qkv(0)
    project_qkv(1)
    project_qkv(2)
    project_qkv(3)
    project_qkv(4)
    project_qkv(5)
    project_qkv(6)
    for j in range(9):
        project_grad(j)
    project_qkv(7)
    project_qkv(8)
    live, live_row, mean, inv_std = st["live"], st["live_row"], st["mean"], st["inv_std"]

    half_rows = ROWS // 2
    row_img = lax.shift_right_logical(
        lax.broadcasted_iota(jnp.int32, (half_rows, half_rows), 0), 3
    )
    col_img = lax.shift_right_logical(
        lax.broadcasted_iota(jnp.int32, (half_rows, half_rows), 1), 3
    )
    same = row_img == col_img
    scale = HD ** (-0.5)
    blocks = [
        (slice(r * half_rows, (r + 1) * half_rows), slice(h * HD, (h + 1) * HD))
        for r in range(2) for h in range(3)
    ]
    qkv = [[acc[i, rs, cols].astype(BF16) for i in range(3)] for rs, cols in blocks]
    ag = [acc[3, rs, cols].astype(BF16) for rs, cols in blocks]
    ok = [same & (live_row[:, rs] > 0.5) for rs, _ in blocks]
    sc = [jnp.where(m, dot(q, k, NT) * scale, -1e30) for m, (q, k, v) in zip(ok, qkv)]
    dprobs = [dot(a, v, NT) for a, (q, k, v) in zip(ag, qkv)]
    ex = [jnp.exp(a - jnp.max(a, axis=1, keepdims=True)) for a in sc]
    probs = [(a / jnp.sum(a, axis=1, keepdims=True)).astype(BF16) for a in ex]
    attn = [dot(p, v).astype(BF16) for p, (q, k, v) in zip(probs, qkv)]
    probs32 = [p.astype(F32) for p in probs]
    inner = [jnp.sum(d * p, axis=1, keepdims=True) for d, p in zip(dprobs, probs32)]
    sg = [(p * (d - n) * scale).astype(BF16) for p, d, n in zip(probs32, dprobs, inner)]
    vg = [dot(p, a, TN).astype(BF16) for p, a in zip(probs, ag)]
    qg = [dot(a, k).astype(BF16) for a, (q, k, v) in zip(sg, qkv)]
    kg = [dot(a, q, TN).astype(BF16) for a, (q, k, v) in zip(sg, qkv)]

    def whole(parts):
        return jnp.concatenate(
            [jnp.concatenate(parts[r * 3 : r * 3 + 3], axis=1) for r in range(2)], axis=0
        )

    grads = [whole(g) for g in (qg, kg, vg)]

    sib_nd, rs_n, sc_d = [], {}, []

    def partial(n):
        for t in range(8):
            rows = slice(t * W + n * 128, t * W + n * 128 + 128)
            p = dot(grads[0], wbuf[0, rows], NT)
            p = p + dot(grads[1], wbuf[1, rows], NT) + dot(grads[2], wbuf[2, rows], NT)
            part_n[t % 2, n, t // 2] = p.astype(BF16)
        if n == 0:
            row_sums()
        sib_nd.append(copy(part_n.at[oc, n], sib_n.at[n], S_NS + n, (dp, tens(0, oc))))

    def fold(n):
        sib_nd[n].wait_recv()
        for k in (2, 1, 3):
            xx = lax.rem(x + k, NX)
            q_n[n, xx] = (part_n[c, n, xx].astype(F32) + sib_n[n, xx].astype(F32)).astype(BF16)
            rs_n[n, k] = copy(
                q_n.at[n, xx], rx_n.at[n, k - 1], S_NX + n * 3 + k - 1, (dp, tens(k, c))
            )

    def row_sums():
        s1, s2 = [], []
        for r in range(2):
            rs = slice(r * half_rows, (r + 1) * half_rows)
            a1s = jnp.zeros((half_rows, HD), F32)
            a2s = jnp.zeros((half_rows, HD), F32)
            for h in range(3):
                cols = slice(h * HD, (h + 1) * HD)
                for i, g in enumerate((qg, kg, vg)):
                    g32 = g[r * 3 + h].astype(F32)
                    a1s = a1s + g32 * jnp.sum(acc[i, ROWS:, cols], axis=0, keepdims=True)
                    a2s = a2s + g32 * acc[i, rs, cols]
            s1.append(jnp.sum(a1s, axis=1, keepdims=True))
            s2.append(jnp.sum(a2s, axis=1, keepdims=True))
        s1r = jnp.sum(jnp.where(eye, jnp.concatenate(s1, axis=0), 0.0), axis=0, keepdims=True)
        s2r = jnp.sum(jnp.where(eye, jnp.concatenate(s2, axis=0), 0.0), axis=0, keepdims=True)
        scal[tn] = jnp.concatenate([s1r, s2r, jnp.zeros((6, ROWS), F32)], axis=0)

    def send_sums():
        own_s = scal.at[tn]
        sc_d.extend([copy(own_s, own_s, S_SC + k - 1, (dp, tens(k, c))) for k in (1, 2, 3)])
        sc_d.extend([copy(own_s, own_s, S_SC + 3 + k, (dp, tens(k, oc))) for k in range(4)])

    partial(0)
    send_sums()
    partial(1)
    fold(0)
    partial(2)
    fold(1)
    fold(2)
    local = xg[tn].astype(F32)
    unit = (local - mean) * inv_std
    for d in sc_d:
        d.wait_recv()
    sums = scal[0]
    for t in range(1, 8):
        sums = sums + scal[t]
    mean1 = jnp.sum(jnp.where(eye, sums[0:1, :], 0.0), axis=1, keepdims=True) * (1.0 / D)
    mean2 = jnp.sum(jnp.where(eye, sums[1:2, :], 0.0), axis=1, keepdims=True) * (1.0 / D)

    r1, r2, rs_o = {}, {}, {}

    def return_z(n):
        lanes = slice(n * 128, n * 128 + 128)
        ng = part_n[c, n, x].astype(F32) + sib_n[n, x].astype(F32)
        for k in (1, 2, 3):
            rs_n[n, k].wait_recv()
            ng = ng + rx_n[n, k - 1].astype(F32)
        back = inv_std * (ng * gain_ref[tn][:, lanes] - mean1 - unit[:, lanes] * mean2)
        moved = jnp.where(live, cot_ref[:, lanes].astype(F32) + back, 0.0).astype(BF16)
        ret1[n] = dot(pick_t[...], moved).astype(BF16).reshape(NZ, 32, 128)
        for k in (8, 7, 9, 6, 10, 5, 11, 4, 12, 3, 13, 2, 14, 1, 15):
            p = lax.rem(z + k, NZ)
            r1[n, k] = copy(ret1.at[n, p], got1.at[n, z], S_R1 + n * 15 + k - 1, (at(k), tn))
        got1[n, z] = ret1[n, z]

    def return_y(n):
        for k in range(1, NZ):
            r1[n, k].wait_recv()
        tiles = got1[n].astype(F32)
        for q in range(NY):
            ret2[n, q] = jnp.concatenate(
                [tiles[s, q * 8 : q * 8 + 8, :] for s in range(NZ)], axis=0
            ).astype(BF16)
        for k in (1, 2, 3):
            p = lax.rem(y + k, NY)
            r2[n, k] = copy(ret2.at[n, p], got2.at[n, y], S_R2 + n * 3 + k - 1, (at(0, k), tn))
        got2[n, y] = ret2[n, y]

    def return_last(n):
        for k in (1, 2, 3):
            r2[n, k].wait_recv()
        pg_ref[:, n * 128 : n * 128 + 128] = dot(
            pack_t[...], got2[n].reshape(512, 128)
        ).astype(BF16)

    return_z(0)
    attn_all = whole(attn)
    for t in range(8):
        part_o[t % 2, t // 2] = dot(attn_all, wbuf[3, t * W : t * W + W], NT).astype(BF16)
    sib_od = copy(part_o.at[oc], sib_o, S_OS, (dp, tens(0, oc)))
    return_z(1)
    return_z(2)
    sib_od.wait_recv()
    for k in (2, 1, 3):
        xx = lax.rem(x + k, NX)
        q_o[xx] = (part_o[c, xx].astype(F32) + sib_o[xx].astype(F32)).astype(BF16)
        rs_o[k] = copy(q_o.at[xx], rx_o.at[k - 1], S_OX + k - 1, (dp, tens(k, c)))
    return_y(0)
    return_y(1)
    branch = part_o[c, x].astype(F32) + sib_o[x].astype(F32)
    for k in (1, 2, 3):
        rs_o[k].wait_recv()
        branch = branch + rx_o[k - 1].astype(F32)
    mixed_ref[...] = jnp.where(live, local + branch, 0.0).astype(BF16)
    return_last(0)
    return_y(2)
    return_last(1)
    return_last(2)
    for d in pending:
        d.wait_send()


def per_device(patches, counts, target, ln_gain, w_qkv, w_out, cotangent):
    images, slot_len, width = patches.shape
    vm = pl.BlockSpec(memory_space=pltpu.VMEM)
    b = lambda *s: pltpu.VMEM(s, BF16)
    f = lambda *s: pltpu.VMEM(s, F32)
    scratch = [
        b(ROWS, W), b(ROWS, W), f(8, 1, W),
        b(4, D, W), b(8, ROWS, W), b(8, ROWS, W), b(NZ, ROWS + 16, SLAB), b(NZ, ROWS, SLAB),
        b(NY, 128, W), b(NY, 128, W), b(NZ, 32, W), b(NZ, 32, W),
        f(NY, 1, 128), f(NY, 1, 128), f(NZ, NY, 1, 128),
        b(ROWS, 512), b(512, ROWS), b(ROWS, 512), f(4, ROWS + 16, W),
        b(2, 3, 4, ROWS, 128), b(2, 4, ROWS, W), b(3, 4, ROWS, 128), b(4, ROWS, W),
        b(3, 4, ROWS, 128), b(4, ROWS, W), b(3, 3, ROWS, 128), b(3, ROWS, W), f(8, 8, ROWS),
        b(3, NZ, 32, 128), b(3, NZ, 32, 128), b(3, NY, 128, 128), b(3, NY, 128, 128),
        pltpu.SemaphoreType.DMA((N_SEM,)), pltpu.SemaphoreType.DMA((N_SEM,)),
        pltpu.SemaphoreType.DMA((6,)),
    ]
    mixed, grad = pl.pallas_call(
        block_kernel,
        out_shape=[pltpu.VMEM((ROWS, W), BF16)] * 2,
        in_specs=[vm] * 2 + [pl.BlockSpec(memory_space=pl.ANY)] * 5,
        out_specs=[vm] * 2,
        scratch_shapes=scratch,
        compiler_params=pltpu.CompilerParams(
            collective_id=0, has_side_effects=True, vmem_limit_bytes=56 << 20
        ),
        name="attention_block",
    )(
        target.reshape(1, images), counts.reshape(1, images), patches.reshape(ROWS, width),
        cotangent.reshape(ROWS, width), ln_gain.reshape(8, 1, W), w_qkv, w_out.T,
    )
    return mixed.reshape(patches.shape), grad.reshape(patches.shape)


def solution(mesh):
    in_specs = (
        P("dp", None, "tensor"), P("dp"), P("dp"), P(), P(None, "dp", "tensor"),
        P("tensor", "dp"), P("dp", None, "tensor"),
    )
    out_specs = (P("dp", None, "tensor"), P("dp", None, "tensor"))
    return jax.shard_map(
        per_device, mesh=mesh, in_specs=in_specs, out_specs=out_specs, check_vma=False
    )
```

```python
import jax
import jax.numpy as jnp
from jax import lax
from jax.experimental import pallas as pl
from jax.experimental.pallas import tpu as pltpu
from jax.sharding import PartitionSpec as P

HD = 128
D = 3072
NZ, NY, NX = 16, 4, 4
ROWS = 256
W = 384
SHARD = 48
SLAB = 192
F32 = jnp.float32
BF16 = jnp.bfloat16
NT = (((1,), (1,)), ((), ()))
TN = (((0,), (0,)), ((), ()))
S_COT = 0
S_XG = 7
S_A1 = 14
S_M1 = 17
S_A2 = 20
S_M2 = 35
S_AY = 50
S_AZR = 53
S_AZL = 60
S_BZR = 68
S_BZL = 76
S_BYR = 83
S_BYL = 99
S_BREL = 115
S_NS = 131
S_NX = 134
S_OS = 143
S_OX = 144
S_SC = 147
S_R1 = 154
S_R2 = 199
N_SEM = 208


def dot(a, b, dims=(((1,), (0,)), ((), ()))):
    return lax.dot_general(a, b, dims, preferred_element_type=F32)


def block_kernel(
    target_ref, counts_ref, x_hbm, cot_hbm, gain_hbm, wqkv_hbm, wout_hbm, mixed_ref, pg_ref,
    x_ref, cot_ref, gain_ref, wbuf, xg, cg, nb, gb, send, mid, mid2, recv, msend, mrecv, mall,
    pick, pick_t, pack_t, acc, part_n, part_o, sib_n, sib_o, q_n, q_o, rx_n, rx_o, scal,
    ret1, got1, ret2, got2, ssem, rsem, lsem,
):
    dp = lax.axis_index("dp")
    tn = lax.axis_index("tensor")
    z, y = lax.div(dp, NY), lax.rem(dp, NY)
    x, c = lax.div(tn, 2), lax.rem(tn, 2)
    oc = 1 - c

    def at(dz=0, dy=0):
        return lax.rem(z + dz + NZ, NZ) * NY + lax.rem(y + dy + NY, NY)

    def tens(dx, core):
        return lax.rem(x + dx, NX) * 2 + core

    def rows_of(p):
        return pl.ds(pl.multiple_of(p * SHARD, SHARD), SHARD)

    def slab(zz):
        return pl.ds(pl.multiple_of(zz * SLAB, SLAB), SLAB)

    barrier = pltpu.get_barrier_semaphore()
    peers = [(at(k, 0), tn) for k in range(1, NZ)]
    peers += [(at(0, k), tn) for k in range(1, NY)]
    peers += [(dp, tens(k, c)) for k in range(1, NX)]
    peers += [(dp, tens(k, oc)) for k in range(NX)]
    for peer in peers:
        pl.semaphore_signal(barrier, inc=1, device_id=peer, device_id_type=pl.DeviceIdType.MESH)
    loads = []
    for i, (a, b) in enumerate((
        (wqkv_hbm, wbuf.at[pl.ds(0, 3), rows_of(dp)]), (wout_hbm, wbuf.at[3, rows_of(dp)]),
        (cot_hbm, cg.at[tn]), (x_hbm, x_ref), (cot_hbm, cot_ref), (gain_hbm, gain_ref),
    )):
        loads.append(pltpu.make_async_copy(a, b, lsem.at[i]))
        loads[-1].start()

    pending = []

    def copy(src, dst, sem, to):
        desc = pltpu.make_async_remote_copy(
            src_ref=src, dst_ref=dst, send_sem=ssem.at[sem], recv_sem=rsem.at[sem],
            device_id=to, device_id_type=pl.DeviceIdType.MESH,
        )
        desc.start()
        pending.append(desc)
        return desc

    eye = lax.broadcasted_iota(jnp.int32, (ROWS, ROWS), 0) == lax.broadcasted_iota(
        jnp.int32, (ROWS, ROWS), 1
    )
    st = {}
    m1, a1 = [], []

    def tiles_sort():
        spread = (
            lax.shift_right_logical(lax.broadcasted_iota(jnp.int32, (32, ROWS), 1), 3)
            == lax.broadcasted_iota(jnp.int32, (32, ROWS), 0)
        ).astype(BF16)
        pair = jnp.concatenate(
            [target_ref[...].astype(F32), counts_ref[...].astype(F32), jnp.zeros((14, 32), F32)],
            axis=0,
        ).astype(BF16)
        pair = dot(pair, spread).astype(jnp.int32)
        lane = lax.broadcasted_iota(jnp.int32, (1, ROWS), 1)
        row = lax.bitwise_and(lane, 7)
        to = pair[0:1, :]
        dest = lax.bitwise_and(to, 3) * 128 + lax.shift_right_logical(to, 2) * 8 + row
        slot = jnp.where(row < pair[1:2, :], lane, -1)
        pack = (lax.broadcasted_iota(jnp.int32, (512, ROWS), 0) == dest).astype(BF16)
        send[...] = dot(pack, x_ref[...]).astype(BF16).reshape(NY, 128, W)
        a_meta = jnp.where(
            lax.broadcasted_iota(jnp.int32, (16, ROWS), 0) == lax.shift_right_logical(dest, 7),
            slot + 1, 0,
        ).astype(F32).astype(BF16)
        b_meta = (
            lax.broadcasted_iota(jnp.int32, (128, ROWS), 0) == lax.bitwise_and(dest, 127)
        ).astype(BF16)
        meta_rows = dot(a_meta, b_meta, NT)
        for k in range(NY):
            msend[k] = meta_rows[k : k + 1, :]
        mid[y] = send[y]
        mrecv[y] = msend[y]
        st["dest"] = dest

    def tiles_first():
        for k in (1, 2, 3):
            p = lax.rem(y + k, NY)
            m1.append(copy(msend.at[p], mrecv.at[y], S_M1 + k - 1, (at(0, k), tn)))
            a1.append(copy(send.at[p], mid.at[y], S_A1 + k - 1, (at(0, k), tn)))

    def tiles_order():
        pack = lax.broadcasted_iota(jnp.int32, (512, ROWS), 0) == st["dest"]
        pack_t[...] = dot(eye.astype(BF16), pack.astype(BF16), NT).astype(BF16)

    for d in loads:
        d.wait()
    pl.semaphore_wait(barrier, len(peers))

    def b_zr(j):
        r = wbuf.at[pl.ds(0, 3), rows_of(at(-j))]
        return copy(r, r, S_BZR + j, (at(1), tn))

    def b_zl(j):
        r = wbuf.at[pl.ds(0, 3), rows_of(at(j))]
        return copy(r, r, S_BZL + j, (at(-1), tn))

    def b_y(d):
        r = wbuf.at[pl.ds(0, 3), rows_of(at(d))]
        return copy(r, r, S_BYR + d, (at(0, 1), tn)), copy(r, r, S_BYL + d, (at(0, -1), tn))

    def b_relay(d, up):
        r = wbuf.at[pl.ds(0, 3), rows_of(at(d, -1 if up else 1))]
        return copy(r, r, S_BREL + d, (at(0, 1 if up else -1), tn))

    def a_zr(j):
        r = wbuf.at[3, slab(lax.rem(z - j + NZ, NZ))]
        return copy(r, r, S_AZR + j, (at(1), tn))

    def a_zl(j):
        r = wbuf.at[3, slab(lax.rem(z + j, NZ))]
        return copy(r, r, S_AZL + j, (at(-1), tn))

    zr, zl, yy, rel, azr, azl = {}, {}, {}, {}, {}, {}
    a_y, a2, m2, cot_d, cot_f, xg_d, xg_f = [], [], [], [], [], [], []

    def tiles_second():
        for d in a1 + m1:
            d.wait_recv()
        tiles = mid[...].astype(F32)
        for q in range(NZ):
            mid2[q] = jnp.concatenate(
                [tiles[s, q * 8 : q * 8 + 8, :] for s in range(NY)], axis=0
            ).astype(BF16)
        recv[z] = mid2[z]
        mall[z] = mrecv[...]

    def tiles_z(*ks):
        for k in ks:
            p = lax.rem(z + k, NZ)
            m2.append(copy(mrecv, mall.at[z], S_M2 + k - 1, (at(k), tn)))
            a2.append(copy(mid2.at[p], recv.at[z], S_A2 + k - 1, (at(k), tn)))

    def tiles_last():
        for d in a2 + m2:
            d.wait_recv()
        lane = lax.broadcasted_iota(jnp.int32, (128, 512), 1)
        sel = (
            lax.broadcasted_iota(jnp.int32, (128, 512), 0) == z * 8 + lax.bitwise_and(lane, 7)
        ).astype(BF16)
        mine = (
            lax.broadcasted_iota(jnp.int32, (64, 512), 0)
            == lax.shift_right_logical(lax.broadcasted_iota(jnp.int32, (64, 512), 1), 3)
        )
        rows = jnp.concatenate([mall[q, s] for q in range(NZ) for s in range(NY)], axis=0)
        where_to = jnp.sum(
            jnp.where(mine, dot(rows.astype(BF16), sel), 0.0), axis=0, keepdims=True
        ).astype(jnp.int32) - 1
        picked = (lax.broadcasted_iota(jnp.int32, (ROWS, 512), 0) == where_to).astype(BF16)
        pick[...] = picked
        xg[tn] = dot(picked, recv[...].reshape(512, W)).astype(BF16)
        xg_d.extend(gather_start(xg, S_XG))

    def tiles_after():
        eye512 = lax.broadcasted_iota(jnp.int32, (512, 512), 0) == lax.broadcasted_iota(
            jnp.int32, (512, 512), 1
        )
        pick_t[...] = dot(eye512.astype(BF16), pick[...], NT).astype(BF16)
        live_col = jnp.sum(pick[...].astype(F32), axis=1, keepdims=True)
        st["live_row"] = jnp.sum(jnp.where(eye, live_col, 0.0), axis=0, keepdims=True)
        st["live"] = live_col > 0.5

    def gather_start(buf, base):
        own = buf.at[tn]
        sib = copy(own, own, base, (dp, tens(0, oc)))
        return [sib] + [copy(own, own, base + k, (dp, tens(k, c))) for k in (1, 2, 3)]

    def gather_pass(buf, base, ds):
        out = []
        for k in (1, 2, 3):
            ds[k].wait_recv()
            r = buf.at[tens(NX - k, c)]
            out.append(copy(r, r, base + 3 + k, (dp, tens(0, oc))))
        return out

    def a_first():
        for k in (1, 2, 3):
            r = wbuf.at[3, rows_of(dp)]
            a_y.append(copy(r, r, S_AY + k - 1, (at(0, k), tn)))

    def b_step(j):
        if j == 0:
            zr[0], zl[0] = b_zr(0), b_zl(0)
            yy[0] = b_y(0)
            return
        zr[j - 1].wait_recv()
        if j < 8:
            zr[j] = b_zr(j)
        yy[NZ - j] = b_y(NZ - j)
        if j < 8:
            zl[j - 1].wait_recv()
            if j < 7:
                zl[j] = b_zl(j)
            yy[j] = b_y(j)

    def relay_step(j):
        if j > 0:
            d = NZ - j
            yy[d][0].wait_recv()
            rel[d] = b_relay(d, True)
        if j < 8:
            yy[j][1].wait_recv()
            rel[j] = b_relay(j, False)

    def a_step(j):
        if j == 0:
            for d in a_y:
                d.wait_recv()
        else:
            azl[j - 1].wait_recv()
            if j < 8:
                azr[j - 1].wait_recv()
        if j < 8:
            azl[j] = a_zl(j)
        if j < 7:
            azr[j] = a_zr(j)

    def b_done(j):
        d = (NZ - j) % NZ
        if j > 0:
            yy[d][1].wait_recv()
            rel[d].wait_recv()
        if j < 8:
            yy[j][0].wait_recv()
            rel[j].wait_recv()

    def project_qkv(j):
        b_done(j)
        for zz in {0: (z,), 8: (lax.rem(z + 8, NZ),)}.get(
            j, (lax.rem(z + j, NZ), lax.rem(z - j + NZ, NZ))
        ):
            rows = nb[zz]
            for i in range(3):
                p = dot(rows, wbuf[i, slab(zz)])
                acc[i] = p if j == 0 else acc[i] + p

    def project_grad(j):
        for zz in {0: (z,), 8: (lax.rem(z + 8, NZ),)}.get(
            j, (lax.rem(z + j, NZ), lax.rem(z - j + NZ, NZ))
        ):
            p = dot(gb[zz], wbuf[3, slab(zz)])
            acc[3, 0:ROWS] = p if j == 0 else acc[3, 0:ROWS] + p

    def grads_ready():
        cot_d[0].wait_recv()
        for d in cot_f:
            d.wait_recv()
        for t in range(8):
            g = jnp.where(st["live"], cg[t], jnp.zeros((), BF16))
            gb[2 * t] = g[:, :SLAB]
            gb[2 * t + 1] = g[:, SLAB:]

    def norm():
        xg_d[0].wait_recv()
        for d in xg_f:
            d.wait_recv()
        total = jnp.zeros((ROWS, 1), F32)
        for t in range(8):
            total = total + jnp.sum(xg[t].astype(F32), axis=1, keepdims=True)
        mean = total * (1.0 / D)
        sq = jnp.zeros((ROWS, 1), F32)
        for t in range(8):
            cen = xg[t].astype(F32) - mean
            sq = sq + jnp.sum(cen * cen, axis=1, keepdims=True)
        inv_std = lax.rsqrt(sq * (1.0 / D) + 1e-06)
        for t in range(8):
            gain = gain_ref[t]
            normed = ((xg[t].astype(F32) - mean) * inv_std * gain).astype(BF16)
            g0 = gain.astype(BF16).astype(F32)
            g1 = (gain - g0).astype(BF16).astype(F32)
            g2 = (gain - g0 - g1).astype(BF16).astype(F32)
            gains = jnp.concatenate([g0, g1, g2, jnp.zeros((13, W), F32)], axis=0).astype(BF16)
            for half in range(2):
                lanes = slice(half * SLAB, (half + 1) * SLAB)
                nb[2 * t + half, 0:ROWS] = normed[:, lanes]
                nb[2 * t + half, ROWS:] = gains[:, lanes]
        st["mean"], st["inv_std"] = mean, inv_std

    def cot_start():
        cot_d.extend(gather_start(cg, S_COT))

    def cot_pass():
        cot_f.extend(gather_pass(cg, S_COT, cot_d))

    def x_pass():
        xg_f.extend(gather_pass(xg, S_XG, xg_d))

    b_step(0)
    a_first()
    cot_start()
    tiles_sort()
    tiles_first()
    b_step(1)
    a_step(0)
    relay_step(0)
    b_step(2)
    a_step(1)
    tiles_second()
    tiles_z(1,15,2,14)
    tiles_z(3,13,4,12)
    relay_step(1)
    b_step(3)
    a_step(2)
    tiles_z(5,11,6,10)
    relay_step(2)
    b_step(4)
    a_step(3)
    tiles_z(7,9,8)
    cot_pass()
    relay_step(3)
    b_step(5)
    a_step(4)
    relay_step(4)
    tiles_last()
    b_step(6)
    a_step(5)
    tiles_after()
    tiles_order()
    relay_step(5)
    b_step(7)
    a_step(6)
    grads_ready()
    relay_step(6)
    x_pass()
    b_step(8)
    a_step(7)
    relay_step(7)
    for j in range(8):
        project_grad(j)
    norm()
    relay_step(8)
    a_step(8)
    project_grad(8)
    project_qkv(0)
    project_qkv(1)
    project_qkv(2)
    project_qkv(3)
    project_qkv(4)
    project_qkv(5)
    project_qkv(6)
    project_qkv(7)
    project_qkv(8)
    live, live_row, mean, inv_std = st["live"], st["live_row"], st["mean"], st["inv_std"]

    half_rows = ROWS // 2
    row_img = lax.shift_right_logical(
        lax.broadcasted_iota(jnp.int32, (half_rows, half_rows), 0), 3
    )
    col_img = lax.shift_right_logical(
        lax.broadcasted_iota(jnp.int32, (half_rows, half_rows), 1), 3
    )
    same = row_img == col_img
    scale = HD ** (-0.5)
    blocks = [
        (slice(r * half_rows, (r + 1) * half_rows), slice(h * HD, (h + 1) * HD))
        for r in range(2) for h in range(3)
    ]
    qkv = [[acc[i, rs, cols].astype(BF16) for i in range(3)] for rs, cols in blocks]
    ag = [acc[3, rs, cols].astype(BF16) for rs, cols in blocks]
    ok = [same & (live_row[:, rs] > 0.5) for rs, _ in blocks]
    sc = [jnp.where(m, dot(q, k, NT) * scale, -1e30) for m, (q, k, v) in zip(ok, qkv)]
    dprobs = [dot(a, v, NT) for a, (q, k, v) in zip(ag, qkv)]
    ex = [jnp.exp(a - jnp.max(a, axis=1, keepdims=True)) for a in sc]
    probs = [(a / jnp.sum(a, axis=1, keepdims=True)).astype(BF16) for a in ex]
    attn = [dot(p, v).astype(BF16) for p, (q, k, v) in zip(probs, qkv)]
    probs32 = [p.astype(F32) for p in probs]
    inner = [jnp.sum(d * p, axis=1, keepdims=True) for d, p in zip(dprobs, probs32)]
    sg = [(p * (d - n) * scale).astype(BF16) for p, d, n in zip(probs32, dprobs, inner)]
    vg = [dot(p, a, TN).astype(BF16) for p, a in zip(probs, ag)]
    qg = [dot(a, k).astype(BF16) for a, (q, k, v) in zip(sg, qkv)]
    kg = [dot(a, q, TN).astype(BF16) for a, (q, k, v) in zip(sg, qkv)]

    def whole(parts):
        return jnp.concatenate(
            [jnp.concatenate(parts[r * 3 : r * 3 + 3], axis=1) for r in range(2)], axis=0
        )

    grads = [whole(g) for g in (qg, kg, vg)]

    sib_nd, rs_n, sc_d = [], {}, []

    def partial(n):
        for t in range(8):
            rows = slice(t * W + n * 128, t * W + n * 128 + 128)
            p = dot(grads[0], wbuf[0, rows], NT)
            p = p + dot(grads[1], wbuf[1, rows], NT) + dot(grads[2], wbuf[2, rows], NT)
            part_n[t % 2, n, t // 2] = p.astype(BF16)
        if n == 0:
            row_sums()
        sib_nd.append(copy(part_n.at[oc, n], sib_n.at[n], S_NS + n, (dp, tens(0, oc))))

    def fold(n):
        sib_nd[n].wait_recv()
        for k in (2, 1, 3):
            xx = lax.rem(x + k, NX)
            q_n[n, xx] = (part_n[c, n, xx].astype(F32) + sib_n[n, xx].astype(F32)).astype(BF16)
            rs_n[n, k] = copy(
                q_n.at[n, xx], rx_n.at[n, k - 1], S_NX + n * 3 + k - 1, (dp, tens(k, c))
            )

    def row_sums():
        s1, s2 = [], []
        for r in range(2):
            rs = slice(r * half_rows, (r + 1) * half_rows)
            a1s = jnp.zeros((half_rows, HD), F32)
            a2s = jnp.zeros((half_rows, HD), F32)
            for h in range(3):
                cols = slice(h * HD, (h + 1) * HD)
                for i, g in enumerate((qg, kg, vg)):
                    g32 = g[r * 3 + h].astype(F32)
                    a1s = a1s + g32 * jnp.sum(acc[i, ROWS:, cols], axis=0, keepdims=True)
                    a2s = a2s + g32 * acc[i, rs, cols]
            s1.append(jnp.sum(a1s, axis=1, keepdims=True))
            s2.append(jnp.sum(a2s, axis=1, keepdims=True))
        s1r = jnp.sum(jnp.where(eye, jnp.concatenate(s1, axis=0), 0.0), axis=0, keepdims=True)
        s2r = jnp.sum(jnp.where(eye, jnp.concatenate(s2, axis=0), 0.0), axis=0, keepdims=True)
        scal[tn] = jnp.concatenate([s1r, s2r, jnp.zeros((6, ROWS), F32)], axis=0)

    def send_sums():
        own_s = scal.at[tn]
        sc_d.extend([copy(own_s, own_s, S_SC + k - 1, (dp, tens(k, c))) for k in (1, 2, 3)])
        sc_d.extend([copy(own_s, own_s, S_SC + 3 + k, (dp, tens(k, oc))) for k in range(4)])

    partial(0)
    send_sums()
    partial(1)
    fold(0)
    partial(2)
    fold(1)
    fold(2)
    local = xg[tn].astype(F32)
    unit = (local - mean) * inv_std
    for d in sc_d:
        d.wait_recv()
    sums = scal[0]
    for t in range(1, 8):
        sums = sums + scal[t]
    mean1 = jnp.sum(jnp.where(eye, sums[0:1, :], 0.0), axis=1, keepdims=True) * (1.0 / D)
    mean2 = jnp.sum(jnp.where(eye, sums[1:2, :], 0.0), axis=1, keepdims=True) * (1.0 / D)

    r1, r2, rs_o = {}, {}, {}

    def return_z(n):
        lanes = slice(n * 128, n * 128 + 128)
        ng = part_n[c, n, x].astype(F32) + sib_n[n, x].astype(F32)
        for k in (1, 2, 3):
            rs_n[n, k].wait_recv()
            ng = ng + rx_n[n, k - 1].astype(F32)
        back = inv_std * (ng * gain_ref[tn][:, lanes] - mean1 - unit[:, lanes] * mean2)
        moved = jnp.where(live, cot_ref[:, lanes].astype(F32) + back, 0.0).astype(BF16)
        ret1[n] = dot(pick_t[...], moved).astype(BF16).reshape(NZ, 32, 128)
        for k in (8, 7, 9, 6, 10, 5, 11, 4, 12, 3, 13, 2, 14, 1, 15):
            p = lax.rem(z + k, NZ)
            r1[n, k] = copy(ret1.at[n, p], got1.at[n, z], S_R1 + n * 15 + k - 1, (at(k), tn))
        got1[n, z] = ret1[n, z]

    def return_y(n):
        for k in range(1, NZ):
            r1[n, k].wait_recv()
        tiles = got1[n].astype(F32)
        for q in range(NY):
            ret2[n, q] = jnp.concatenate(
                [tiles[s, q * 8 : q * 8 + 8, :] for s in range(NZ)], axis=0
            ).astype(BF16)
        for k in (1, 2, 3):
            p = lax.rem(y + k, NY)
            r2[n, k] = copy(ret2.at[n, p], got2.at[n, y], S_R2 + n * 3 + k - 1, (at(0, k), tn))
        got2[n, y] = ret2[n, y]

    def return_last(n):
        for k in (1, 2, 3):
            r2[n, k].wait_recv()
        pg_ref[:, n * 128 : n * 128 + 128] = dot(
            pack_t[...], got2[n].reshape(512, 128)
        ).astype(BF16)

    return_z(0)
    attn_all = whole(attn)
    for t in range(8):
        part_o[t % 2, t // 2] = dot(attn_all, wbuf[3, t * W : t * W + W], NT).astype(BF16)
    sib_od = copy(part_o.at[oc], sib_o, S_OS, (dp, tens(0, oc)))
    return_z(1)
    return_z(2)
    sib_od.wait_recv()
    for k in (2, 1, 3):
        xx = lax.rem(x + k, NX)
        q_o[xx] = (part_o[c, xx].astype(F32) + sib_o[xx].astype(F32)).astype(BF16)
        rs_o[k] = copy(q_o.at[xx], rx_o.at[k - 1], S_OX + k - 1, (dp, tens(k, c)))
    return_y(0)
    return_y(1)
    branch = part_o[c, x].astype(F32) + sib_o[x].astype(F32)
    for k in (1, 2, 3):
        rs_o[k].wait_recv()
        branch = branch + rx_o[k - 1].astype(F32)
    mixed_ref[...] = jnp.where(live, local + branch, 0.0).astype(BF16)
    return_last(0)
    return_y(2)
    return_last(1)
    return_last(2)
    for d in pending:
        d.wait_send()


def per_device(patches, counts, target, ln_gain, w_qkv, w_out, cotangent):
    images, slot_len, width = patches.shape
    vm = pl.BlockSpec(memory_space=pltpu.VMEM)
    b = lambda *s: pltpu.VMEM(s, BF16)
    f = lambda *s: pltpu.VMEM(s, F32)
    scratch = [
        b(ROWS, W), b(ROWS, W), f(8, 1, W),
        b(4, D, W), b(8, ROWS, W), b(8, ROWS, W), b(NZ, ROWS + 16, SLAB), b(NZ, ROWS, SLAB),
        b(NY, 128, W), b(NY, 128, W), b(NZ, 32, W), b(NZ, 32, W),
        f(NY, 1, 128), f(NY, 1, 128), f(NZ, NY, 1, 128),
        b(ROWS, 512), b(512, ROWS), b(ROWS, 512), f(4, ROWS + 16, W),
        b(2, 3, 4, ROWS, 128), b(2, 4, ROWS, W), b(3, 4, ROWS, 128), b(4, ROWS, W),
        b(3, 4, ROWS, 128), b(4, ROWS, W), b(3, 3, ROWS, 128), b(3, ROWS, W), f(8, 8, ROWS),
        b(3, NZ, 32, 128), b(3, NZ, 32, 128), b(3, NY, 128, 128), b(3, NY, 128, 128),
        pltpu.SemaphoreType.DMA((N_SEM,)), pltpu.SemaphoreType.DMA((N_SEM,)),
        pltpu.SemaphoreType.DMA((6,)),
    ]
    mixed, grad = pl.pallas_call(
        block_kernel,
        out_shape=[pltpu.VMEM((ROWS, W), BF16)] * 2,
        in_specs=[vm] * 2 + [pl.BlockSpec(memory_space=pl.ANY)] * 5,
        out_specs=[vm] * 2,
        scratch_shapes=scratch,
        compiler_params=pltpu.CompilerParams(
            collective_id=0, has_side_effects=True, vmem_limit_bytes=56 << 20
        ),
        name="attention_block",
    )(
        target.reshape(1, images), counts.reshape(1, images), patches.reshape(ROWS, width),
        cotangent.reshape(ROWS, width), ln_gain.reshape(8, 1, W), w_qkv, w_out.T,
    )
    return mixed.reshape(patches.shape), grad.reshape(patches.shape)


def solution(mesh):
    in_specs = (
        P("dp", None, "tensor"), P("dp"), P("dp"), P(), P(None, "dp", "tensor"),
        P("tensor", "dp"), P("dp", None, "tensor"),
    )
    out_specs = (P("dp", None, "tensor"), P("dp", None, "tensor"))
    return jax.shard_map(
        per_device, mesh=mesh, in_specs=in_specs, out_specs=out_specs, check_vma=False
    )
```
